32 devices in a mesh: groups: 2 (over x), dp: 8 (over z, y), tensor: 2 (over core).
Axes of the slice: x: 2, y: 2, z: 4, core: 2. Of those that a mesh axis runs over, the one named last changes fastest.
Arguments:
- visual_tokens: bfloat16 [7680, 8192], P(('groups', 'dp'), 'tensor'), parts along dimension 0, may hold values from -800 to 800
- kv_weight: bfloat16 [2, 4096, 2, 512], P('tensor'), may hold values from -0.0625 to 0.0625
- image_lengths: int32 [16, 12], P('groups'), parts along dimension 0, may hold values from 1 to 48, 480 in all within a row
- image_owner: int32 [192], P('groups'), parts along dimension 0, may hold values from 0 to 191, as said below
- cache_lengths: int32 [384], P(('groups', 'dp')), parts along dimension 0, may hold values from 2 to 128
- cache_keys: bfloat16 [384, 128, 512], P(('groups', 'dp'), None, 'tensor'), parts along dimension 0, may hold values from -4.5 to 4.5
- cache_values: bfloat16 [384, 128, 512], P(('groups', 'dp'), None, 'tensor'), parts along dimension 0, may hold values from -4 to 4
- step_queries: bfloat16 [384, 4, 4096], P(('groups', 'dp'), None, 'tensor'), parts along dimension 0, may hold values from -30 to 30
- step_keys: bfloat16 [384, 4, 512], P(('groups', 'dp'), None, 'tensor'), parts along dimension 0, may hold values from -4 to 4
- step_values: bfloat16 [384, 4, 512], P(('groups', 'dp'), None, 'tensor'), parts along dimension 0, may hold values from -4 to 4
Outputs:
- attended: bfloat16 [384, 4, 4096], P(('groups', 'dp'), None, 'tensor'), parts along dimension 0
The draws below stay inside these ranges and needn't reach their ends.
There are 2 independent parts, one for each index of `groups`. The reference program is written for one: setup_inputs(seed, part) draws one part's arguments, and reference() takes and returns one part's arrays. A program takes and returns all parts, laid end to end along the dimension named above; an argument that names none is the same for every part. Nothing has to cross between parts.
Inputs may be any that keep to these rules, and one draw needn't show every extreme that they name: `image_owner`: distinct rows. The images of one source dp index reach at most 3 rows of any one dp index (rows of dp index k: k * 24 to (k + 1) * 24 - 1), and some source reaches 3; some dp index owns 24 screenshots and some own none.
All inputs are finite; a program needn't handle non-finite values.
Results may differ from the reference program's by a relative error of at most 0.0053.
Values may be sent and summed in bfloat16 or wider, within the bound.
No kernel may reach another device: no remote copies, remote signals or barrier semaphores. Data moves between devices by JAX's collectives and lax.ppermute only.
A program may use at most 128 MiB of HBM per device.

```python
import math
import jax
import jax.numpy as jnp
import numpy as np
from jax import lax

D = 8192
HD = 128
QH = 32
KVH = 4
STEPS = 4
VMAX = 48
CTX = 128
IMG_DEV = 12
ROWS_DEV = 24
V_DEV = 480
SOURCES = 8
NIMG = 96
ROWS = 192
VTOK = 3840
N_TENSOR = 2


def draw_image_owner(key, part):
    key = jax.random.fold_in(key, 11)
    subkeys = jax.random.split(key, 5)
    device_count = SOURCES
    half_count = device_count // 2
    pairing = jax.random.permutation(subkeys[0], device_count)
    shifted = jax.random.randint(subkeys[1], (half_count,), 0, IMG_DEV + 1)
    shifted = shifted.at[0].set(IMG_DEV)
    owner_load = jnp.zeros((device_count,), jnp.int32)
    owner_load = owner_load.at[pairing[:half_count]].set(IMG_DEV + shifted)
    owner_load = owner_load.at[pairing[half_count:]].set(IMG_DEV - shifted)
    run_order = jax.random.permutation(subkeys[2], device_count)
    ordered = owner_load[run_order]
    run_ends = jnp.cumsum(ordered)
    begins = run_ends - ordered
    slot_ids = jnp.arange(NIMG, dtype=jnp.int32)
    position = jnp.sum((run_ends[None, :] <= slot_ids[:, None]).astype(jnp.int32), axis=1)
    owner_index = run_order[position]
    run_rank = slot_ids - begins[position]
    rotation = jax.random.randint(subkeys[3], (device_count,), 0, ROWS_DEV)
    row_offset = (run_rank + rotation[owner_index]) % ROWS_DEV
    sources = jax.random.permutation(subkeys[4], device_count)
    image_id = sources[slot_ids % device_count] * IMG_DEV + slot_ids // device_count
    return jnp.zeros((NIMG,), jnp.int32).at[image_id].set(owner_index * ROWS_DEV + row_offset)


def draw_cache_lengths(key, part):
    key = jax.random.fold_in(key, 23)
    subkeys = jax.random.split(key, 2)
    lengths = jax.random.randint(subkeys[0], (ROWS,), 2, CTX + 1)
    longest = jax.random.randint(subkeys[1], (), 0, ROWS)
    return lengths.at[longest].set(CTX).astype(jnp.int32)


def draw_visual_tokens(key, part):
    key = jax.random.fold_in(key, 37)
    subkeys = jax.random.split(key, 3)
    columns = jnp.arange(D, dtype=jnp.float32) / D
    column_scale = 10.0 ** columns * jax.random.uniform(subkeys[0], (D,), jnp.float32, 0.6, 1.6)
    row_scale = jnp.exp(jax.random.uniform(subkeys[1], (VTOK,), jnp.float32, 0.0, 2.3))
    entries = jax.random.truncated_normal(subkeys[2], -4.0, 4.0, (VTOK, D), jnp.float32)
    return (entries * row_scale[:, None] * column_scale[None, :]).astype(jnp.bfloat16)


def draw_cache_keys(key, part):
    key = jax.random.fold_in(key, 41)
    entries = jax.random.truncated_normal(key, -4.0, 4.0, (ROWS, CTX, KVH * HD), jnp.float32)
    return entries.astype(jnp.bfloat16)


def draw_step_queries(key, part):
    key = jax.random.fold_in(key, 53)
    entries = jax.random.truncated_normal(key, -4.0, 4.0, (ROWS, STEPS, QH * HD), jnp.float32)
    return entries.astype(jnp.bfloat16)


def shard_levels(key, extent, cuts, least, largest):
    def one(axis_at, blocks):
        draws = jax.random.uniform(jax.random.fold_in(jax.random.fold_in(key, 6), axis_at), (blocks,), jnp.float32, least / len(cuts), largest / len(cuts))
        return jnp.repeat(jnp.exp(draws), extent[axis_at] // blocks).reshape((-1,) + (1,) * (len(extent) - axis_at - 1))

    factor_of = one(*cuts[0])
    for cut in cuts[1:]:
        factor_of = factor_of * one(*cut)
    return factor_of


def length_profile(amount, total, reach, slope):
    weights = [(1 << 20) // math.isqrt(grade ** slope) + 1 for grade in range(2, amount + 1)]
    spare, counts = total - reach - (amount - 1), [1] * (amount - 1)
    while spare > 0:
        movable = [i for i in range(amount - 1) if counts[i] < reach]
        pool, remaining = sum([weights[i] for i in movable]), spare
        for i in movable:
            more = min(reach - counts[i], max(1, remaining * weights[i] // pool), spare)
            counts[i] = counts[i] + more
            spare = spare - more
    return np.array([reach] + counts)


def ragged(rng, number_of, total, most, slope):
    if number_of == 2:
        one = jax.random.randint(rng, (), max(1, total - most), min(most, total - 1) + 1)
        return jnp.stack([one, total - one])
    sizes = jnp.asarray(length_profile(number_of, total, most, slope), jnp.int32)
    pairs = (number_of - 1) // 2
    giver, receiver = sizes[1:1 + 2 * pairs:2], sizes[2:2 + 2 * pairs:2]
    slack = jnp.minimum(giver - 1, most - receiver)
    moved = jax.random.randint(jax.random.fold_in(rng, 1), (pairs,), 0, 1 << 20) % (slack + 1)
    sizes = sizes.at[1:1 + 2 * pairs:2].set(giver - moved).at[2:2 + 2 * pairs:2].set(receiver + moved)
    return sizes[jax.random.permutation(jax.random.fold_in(rng, 2), number_of)]


def noise(stream_key, extent, width, reach, pieces=(), kind=jnp.bfloat16):
    values = width * jax.random.normal(stream_key, extent, jnp.float32)
    if pieces:
        values = values * shard_levels(stream_key, extent, pieces, -0.22, 0.18)
    return jnp.clip(values, -reach, reach).astype(kind)


def setup_inputs(seed: int = 0, part: int = 0) -> dict:
    streams_of = jax.random.split(jax.random.key(seed), 11)
    part_splits = jax.random.split(jax.random.fold_in(streams_of[10], part), 11)
    visual_tokens = draw_visual_tokens(jax.random.fold_in(jax.random.fold_in(streams_of[10], part), 71), part)
    kv_weight = noise(streams_of[1], (N_TENSOR, D // N_TENSOR, 2, KVH * HD), D ** -0.5, 0.0625, ((0, 2),))
    image_lengths = jax.vmap(lambda own: ragged(own, IMG_DEV, V_DEV, VMAX, 1))(jax.random.split(part_splits[2], SOURCES)).reshape((SOURCES, IMG_DEV)).astype(jnp.int32)
    image_owner = draw_image_owner(jax.random.fold_in(jax.random.fold_in(streams_of[10], part), 71), part)
    cache_lengths = draw_cache_lengths(jax.random.fold_in(jax.random.fold_in(streams_of[10], part), 71), part)
    cache_keys = draw_cache_keys(jax.random.fold_in(jax.random.fold_in(streams_of[10], part), 71), part)
    cache_values = noise(part_splits[6], (ROWS, CTX, KVH * HD), 1.0, 4.0, ((0, 8), (2, 2)))
    step_queries = draw_step_queries(jax.random.fold_in(jax.random.fold_in(streams_of[10], part), 71), part)
    step_keys = noise(part_splits[8], (ROWS, STEPS, KVH * HD), 1.0, 4.0, ((0, 8), (2, 2)))
    step_values = noise(part_splits[9], (ROWS, STEPS, KVH * HD), 1.0, 4.0, ((0, 8), (2, 2)))
    return dict(visual_tokens=visual_tokens, kv_weight=kv_weight, image_lengths=image_lengths, image_owner=image_owner, cache_lengths=cache_lengths, cache_keys=cache_keys, cache_values=cache_values, step_queries=step_queries, step_keys=step_keys, step_values=step_values)


EPSILON = 1e-06

def reference(visual_tokens, kv_weight, image_lengths, image_owner, cache_lengths, cache_keys, cache_values, step_queries, step_keys, step_values):
    features = visual_tokens.astype(jnp.float32)
    squares = lax.optimization_barrier(jnp.mean(features * features, axis=1, keepdims=True))
    normed = (features * lax.rsqrt(squares + EPSILON)).astype(jnp.bfloat16)
    weight = kv_weight.reshape(D, 2 * KVH * HD)
    projected = jnp.dot(normed, weight, preferred_element_type=jnp.float32).astype(jnp.bfloat16)
    projected = projected.reshape(-1, 2, KVH * HD)
    image_starts = jnp.cumsum(image_lengths, axis=1) - image_lengths
    image_starts = (image_starts + jnp.arange(SOURCES, dtype=jnp.int32)[:, None] * V_DEV).reshape(-1).astype(jnp.int32)
    flat_lengths = image_lengths.reshape(-1).astype(jnp.int32)
    total_rows = cache_lengths.shape[0]
    image_of_row = jnp.full((total_rows,), -1, jnp.int32).at[image_owner].set(jnp.arange(NIMG, dtype=jnp.int32))
    has_image = image_of_row >= 0
    safe_image = jnp.maximum(image_of_row, 0)
    visual_length = jnp.where(has_image, flat_lengths[safe_image], 0).astype(jnp.int32)
    offsets = jnp.arange(VMAX, dtype=jnp.int32)
    token_index = jnp.clip(image_starts[safe_image][:, None] + offsets[None, :], 0, projected.shape[0] - 1).astype(jnp.int32)
    visual_pairs = projected[token_index]
    group_size = QH // KVH
    queries = step_queries.astype(jnp.float32).reshape(total_rows, STEPS, KVH, group_size, HD)
    all_keys = jnp.concatenate([cache_keys, visual_pairs[:, :, 0, :], step_keys], axis=1)
    all_values = jnp.concatenate([cache_values, visual_pairs[:, :, 1, :], step_values], axis=1)
    all_keys = all_keys.astype(jnp.float32).reshape(total_rows, -1, KVH, HD)
    all_values = all_values.astype(jnp.float32).reshape(total_rows, -1, KVH, HD)
    scores = jnp.einsum('rsgjd,rpgd->rgjsp', queries, all_keys) * HD ** (-0.5)
    key_span = all_keys.shape[1]
    position = jnp.arange(key_span, dtype=jnp.int32)
    live_cache = position[None, :] < cache_lengths[:, None]
    visual_place = position - CTX
    live_visual = (visual_place[None, :] >= 0) & (visual_place[None, :] < visual_length[:, None])
    step_place = position - CTX - VMAX
    live_step = (step_place[None, :] >= 0) & (step_place[None, :] <= jnp.arange(STEPS, dtype=jnp.int32)[:, None])
    allowed = (live_cache | live_visual)[:, None, None, None, :] | live_step[None, None, None, :, :]
    masked = jnp.where(allowed, scores, -1e+30)
    row_peak = lax.optimization_barrier(jnp.max(masked, axis=-1, keepdims=True))
    weights = jnp.where(allowed, jnp.exp(masked - row_peak), 0.0)
    weights = (weights / lax.optimization_barrier(jnp.sum(weights, axis=-1, keepdims=True))).astype(jnp.bfloat16)
    mixed = jnp.einsum('rgjsp,rpgd->rsgjd', weights.astype(jnp.float32), all_values)
    return mixed.astype(jnp.bfloat16).reshape(total_rows, STEPS, QH * HD)
```

```python
import jax
import jax.numpy as jnp
from jax import lax
from jax.experimental import pallas as pl
from jax.experimental.pallas import tpu as pltpu
from jax.sharding import PartitionSpec as P

D = 8192
HD = 128
STEPS = 4
VMAX = 48
EPSILON = 1e-06
LANES = 128
FLOOR = -1e30
VMEM_BYTES = 40 << 20


def dot_t(a, b):
    return lax.dot_general(a, b, (((1,), (1,)), ((), ())), preferred_element_type=jnp.float32)


def dot(a, b):
    return jnp.dot(a, b, preferred_element_type=jnp.float32)


def pack_queries(image_owner, step_queries, devices, capacity):
    rows = step_queries.shape[0]
    images = image_owner.shape[0] // devices
    slots = devices * capacity

    def kernel(owner, queries, packed, slot_of_row, row_of_slot, sems):
        base = lax.axis_index("dp") * rows
        for r in range(rows):
            slot_of_row[r] = -1
        copies = []
        for s in range(devices):
            for k in range(capacity):
                row_of_slot[s * capacity + k] = 0
            rank = jnp.int32(0)
            for i in range(images):
                row = owner[s * images + i] - base
                local = jnp.logical_and(row >= 0, row < rows)
                slot = s * capacity + rank
                row_of_slot[jnp.where(local, slot, slots)] = row
                slot_of_row[jnp.where(local, row, rows)] = slot
                rank = rank + local.astype(jnp.int32)
            for k in range(capacity):
                slot = s * capacity + k
                copy = pltpu.make_async_copy(
                    queries.at[row_of_slot[slot]], packed.at[slot], sems.at[slot]
                )
                copy.start()
                copies.append(copy)
        for copy in copies:
            copy.wait()

    return pl.pallas_call(
        kernel,
        in_specs=[
            pl.BlockSpec(memory_space=pltpu.SMEM),
            pl.BlockSpec(memory_space=pl.ANY),
        ],
        out_specs=[
            pl.BlockSpec(memory_space=pl.ANY),
            pl.BlockSpec(memory_space=pltpu.SMEM),
        ],
        out_shape=[
            jax.ShapeDtypeStruct((slots,) + step_queries.shape[1:], step_queries.dtype),
            jax.ShapeDtypeStruct((rows + 1,), jnp.int32),
        ],
        scratch_shapes=[
            pltpu.SMEM((slots + 1,), jnp.int32),
            pltpu.SemaphoreType.DMA((slots,)),
        ],
        name="pack_queries",
    )(image_owner, step_queries)


def project(tokens, weight, half, with_squares):
    count, depth = tokens.shape
    width = weight.shape[2] // 2
    chunk = 512
    columns = 2 * width + (LANES if with_squares else 0)

    def kernel(half_ref, token_ref, weight_ref, out_ref):
        total = jnp.zeros((count, 2 * width), jnp.float32)
        squares = jnp.zeros((count, LANES), jnp.float32)
        for at in range(0, depth, chunk):
            x = token_ref[:, at : at + chunk]
            w = jnp.swapaxes(weight_ref[at : at + chunk], 0, 1)
            total += dot(x, jnp.concatenate([w[0], w[1]], axis=1))
            if with_squares:
                for lane in range(0, chunk, LANES):
                    wide = x[:, lane : lane + LANES].astype(jnp.float32)
                    squares += wide * wide
        out_ref[:, : 2 * width] = total
        if with_squares:
            out_ref[:, 2 * width :] = jnp.broadcast_to(
                jnp.sum(squares, axis=1, keepdims=True), (count, LANES)
            )

    return pl.pallas_call(
        kernel,
        grid_spec=pltpu.PrefetchScalarGridSpec(
            num_scalar_prefetch=1,
            grid=(1,),
            in_specs=[
                pl.BlockSpec((count, depth), lambda i, half_ref: (0, 0)),
                pl.BlockSpec((depth, 2, width), lambda i, half_ref: (0, 0, half_ref[0])),
            ],
            out_specs=pl.BlockSpec((count, columns), lambda i, half_ref: (0, 0)),
        ),
        out_shape=jax.ShapeDtypeStruct((count, columns), jnp.float32),
        compiler_params=pltpu.CompilerParams(vmem_limit_bytes=VMEM_BYTES),
        cost_estimate=pl.CostEstimate(
            flops=4 * count * depth * width,
            bytes_accessed=2 * depth * (count + 2 * width),
            transcendentals=0,
        ),
        name="project_partner" if with_squares else "project_own",
    )(half.reshape(1), tokens, weight)


def stack_heads(read, store, heads):
    for j in range(heads):
        store(j * STEPS, read(j).astype(jnp.float32))


def cached_attention(queries, cache_keys, cache_values, step_keys, step_values, lengths):
    rows, context, width = cache_keys.shape
    kv_local = width // HD
    heads = queries.shape[2] // HD
    group = heads // kv_local
    stacked = group * STEPS
    block = 8 if rows % 8 == 0 else 1
    scale = HD**-0.5

    def kernel(length_ref, q_ref, k_ref, v_ref, sk_ref, sv_ref, out_ref, log_ref, q_s, sk_s, sv_s):
        first = pl.program_id(0) * block
        for r in range(block):
            for g in range(kv_local):
                sk_s[g, r * STEPS : (r + 1) * STEPS, :] = sk_ref[
                    r, :, g * HD : (g + 1) * HD
                ].astype(jnp.float32)
                sv_s[g, r * STEPS : (r + 1) * STEPS, :] = sv_ref[
                    r, :, g * HD : (g + 1) * HD
                ].astype(jnp.float32)
                for j in range(group):
                    h = g * group + j
                    at = r * stacked + j * STEPS
                    q_s[g, at : at + STEPS, :] = q_ref[r, :, h * HD : (h + 1) * HD].astype(
                        jnp.float32
                    )
        lane = lax.broadcasted_iota(jnp.int32, (STEPS, LANES), 1)
        logs = [jnp.zeros((STEPS, LANES), jnp.float32) for _ in range(block)]
        for g in range(kv_local):
            q = q_s[g].astype(jnp.bfloat16)
            steps = dot_t(q, sk_s[g].astype(jnp.bfloat16)) * scale
            at_row = lax.broadcasted_iota(jnp.int32, steps.shape, 0)
            at_key = lax.broadcasted_iota(jnp.int32, steps.shape, 1)
            own = (at_row // stacked == at_key // STEPS) & (at_key % STEPS <= at_row % STEPS)
            steps = jnp.where(own, steps, FLOOR)
            step_peak = jnp.max(steps, axis=1, keepdims=True)
            scores = []
            position = lax.broadcasted_iota(jnp.int32, (stacked, context), 1)
            for r in range(block):
                part = dot_t(q[r * stacked : (r + 1) * stacked], k_ref[r, :, g * HD : (g + 1) * HD])
                scores.append(jnp.where(position < length_ref[first + r], part * scale, FLOOR))
            cached = jnp.concatenate(scores, axis=0)
            peak = jnp.maximum(jnp.max(cached, axis=1, keepdims=True), step_peak)
            cached = jnp.exp(cached - peak)
            steps = jnp.where(own, jnp.exp(steps - peak), 0.0)
            total = jnp.sum(cached, axis=1, keepdims=True) + jnp.sum(steps, axis=1, keepdims=True)
            cached = cached.astype(jnp.bfloat16)
            mixed = dot(steps.astype(jnp.bfloat16), sv_s[g].astype(jnp.bfloat16))
            inverse = 1.0 / total
            log = jnp.broadcast_to(peak + jnp.log(total), (block * stacked, LANES))
            for r in range(block):
                span = slice(r * stacked, (r + 1) * stacked)
                part = dot(cached[span], v_ref[r, :, g * HD : (g + 1) * HD])
                part = (part + mixed[span]) * inverse[span]
                for j in range(group):
                    h = g * group + j
                    head = slice(j * STEPS, (j + 1) * STEPS)
                    out_ref[r, :, h * HD : (h + 1) * HD] = part[head]
                    at = r * stacked + j * STEPS
                    logs[r] = jnp.where(lane == h, log[at : at + STEPS], logs[r])
        for r in range(block):
            log_ref[r] = logs[r]

    def spec(array):
        return pl.BlockSpec((block,) + array.shape[1:], lambda i, length_ref: (i, 0, 0))

    return pl.pallas_call(
        kernel,
        grid_spec=pltpu.PrefetchScalarGridSpec(
            num_scalar_prefetch=1,
            grid=(rows // block,),
            in_specs=[
                spec(queries),
                spec(cache_keys),
                spec(cache_values),
                spec(step_keys),
                spec(step_values),
            ],
            out_specs=[
                spec(queries),
                pl.BlockSpec((block, STEPS, LANES), lambda i, length_ref: (i, 0, 0)),
            ],
            scratch_shapes=[
                pltpu.VMEM((kv_local, block * stacked, HD), jnp.float32),
                pltpu.VMEM((kv_local, block * STEPS, HD), jnp.float32),
                pltpu.VMEM((kv_local, block * STEPS, HD), jnp.float32),
            ],
        ),
        out_shape=[
            jax.ShapeDtypeStruct(queries.shape, jnp.float32),
            jax.ShapeDtypeStruct((rows, STEPS, LANES), jnp.float32),
        ],
        compiler_params=pltpu.CompilerParams(vmem_limit_bytes=VMEM_BYTES),
        cost_estimate=pl.CostEstimate(
            flops=4 * rows * heads * STEPS * HD * context,
            bytes_accessed=4 * rows * context * width,
            transcendentals=rows * heads * STEPS * context,
        ),
        name="cached_attention",
    )(lengths, queries, cache_keys, cache_values, step_keys, step_values)


def visual_attention(places, queries, pairs):
    images = places.shape[1]
    slots, _, full = queries.shape
    heads = full // HD
    kv_local = pairs.shape[1] // (2 * HD)
    group = heads // kv_local
    stacked = group * STEPS
    window = VMAX + 16
    scale = HD**-0.5

    def kernel(place_ref, q_ref, pair_ref, out_ref, q_s, score_s, weight_s):
        for i in range(images):
            slot = place_ref[0, i]
            for h in range(heads):
                q_s[i, h * STEPS : (h + 1) * STEPS, :] = q_ref[
                    slot, :, h * HD : (h + 1) * HD
                ].astype(jnp.float32)
        for i in range(images):
            rows = pl.ds(pl.multiple_of(place_ref[1, i], 16), window)
            q = q_s[i].astype(jnp.bfloat16)
            for g in range(kv_local):
                score_s[i, g * stacked : (g + 1) * stacked, :] = dot_t(
                    q[g * stacked : (g + 1) * stacked], pair_ref[rows, g * HD : (g + 1) * HD]
                )
        column = lax.broadcasted_iota(jnp.int32, (heads * STEPS, window), 1)
        inverses = []
        logs = []
        for i in range(images):
            start = place_ref[2, i]
            live = (column >= start) & (column < start + place_ref[3, i])
            scores = jnp.where(live, score_s[i] * scale, FLOOR)
            peak = jnp.max(scores, axis=1, keepdims=True)
            weights = jnp.exp(scores - peak)
            total = jnp.sum(weights, axis=1, keepdims=True)
            weight_s[i] = weights.astype(jnp.bfloat16)
            inverses.append(1.0 / total)
            logs.append(jnp.broadcast_to(peak + jnp.log(total), (heads * STEPS, LANES)))
        lane = lax.broadcasted_iota(jnp.int32, (STEPS, LANES), 1)
        for i in range(images):
            slot = place_ref[0, i]
            rows = pl.ds(pl.multiple_of(place_ref[1, i], 16), window)
            high_part = jnp.zeros((STEPS, LANES), jnp.float32)
            for g in range(kv_local):
                at = (kv_local + g) * HD
                part = dot(
                    weight_s[i, g * stacked : (g + 1) * stacked, :], pair_ref[rows, at : at + HD]
                )
                part = part * inverses[i][g * stacked : (g + 1) * stacked]
                for j in range(group):
                    h = g * group + j
                    out_ref[slot, :, h * HD : (h + 1) * HD] = part[
                        j * STEPS : (j + 1) * STEPS
                    ].astype(out_ref.dtype)
            packed = jnp.zeros((STEPS, LANES), jnp.float32)
            for h in range(heads):
                log = logs[i][h * STEPS : (h + 1) * STEPS]
                packed = jnp.where(lane % heads == h, log, packed)
            first = packed.astype(jnp.bfloat16).astype(jnp.float32)
            rest = packed - first
            second = rest.astype(jnp.bfloat16).astype(jnp.float32)
            third = rest - second
            out_ref[slot, :, full:] = jnp.where(
                lane < heads,
                first,
                jnp.where(lane < 2 * heads, second, jnp.where(lane < 3 * heads, third, 0.0)),
            ).astype(out_ref.dtype)

    vmem = pl.BlockSpec(memory_space=pltpu.VMEM)
    return pl.pallas_call(
        kernel,
        in_specs=[pl.BlockSpec(memory_space=pltpu.SMEM), vmem, vmem],
        out_specs=vmem,
        out_shape=jax.ShapeDtypeStruct((slots, STEPS, full + LANES), queries.dtype),
        scratch_shapes=[
            pltpu.VMEM((images, heads * STEPS, HD), jnp.float32),
            pltpu.VMEM((images, heads * STEPS, window), jnp.float32),
            pltpu.VMEM((images, heads * STEPS, window), jnp.bfloat16),
        ],
        compiler_params=pltpu.CompilerParams(vmem_limit_bytes=VMEM_BYTES),
        name="visual_attention",
    )(places, queries, pairs)


def merge(slot_of_row, returned, cached, cached_log):
    rows, _, full = cached.shape
    heads = full // HD

    def kernel(slot_ref, returned_ref, cached_ref, log_ref, out_ref):
        for r in range(rows):
            slot = slot_ref[r]
            present = slot >= 0
            slot = jnp.maximum(slot, 0)
            terms = returned_ref[slot, :, full:].astype(jnp.float32)
            for h in range(heads):
                log = (
                    terms[:, h : h + 1]
                    + terms[:, heads + h : heads + h + 1]
                    + terms[:, 2 * heads + h : 2 * heads + h + 1]
                )
                share = 1.0 / (1.0 + jnp.exp(log_ref[r, :, h : h + 1] - log))
                own = cached_ref[r, :, h * HD : (h + 1) * HD]
                other = returned_ref[slot, :, h * HD : (h + 1) * HD].astype(jnp.float32)
                mixed = own + jnp.where(present, share * (other - own), 0.0)
                out_ref[r, :, h * HD : (h + 1) * HD] = mixed.astype(out_ref.dtype)

    vmem = pl.BlockSpec(memory_space=pltpu.VMEM)
    return pl.pallas_call(
        kernel,
        in_specs=[pl.BlockSpec(memory_space=pltpu.SMEM), vmem, vmem, vmem],
        out_specs=vmem,
        out_shape=jax.ShapeDtypeStruct(cached.shape, jnp.bfloat16),
        compiler_params=pltpu.CompilerParams(vmem_limit_bytes=VMEM_BYTES),
        name="merge",
    )(slot_of_row, returned, cached, cached_log)


def shards(
    visual_tokens,
    kv_weight,
    image_lengths,
    image_owner,
    cache_lengths,
    cache_keys,
    cache_values,
    step_queries,
    step_keys,
    step_values,
):
    devices = lax.axis_size("dp")
    rows_local = cache_lengths.shape[0]
    images_local = image_lengths.shape[1]
    capacity = -(-rows_local // devices)
    width_local = cache_keys.shape[2]
    weight_half = kv_weight[0]
    tensor = lax.axis_index("tensor").astype(jnp.int32)

    packed, slot_of_row = pack_queries(image_owner, step_queries, devices, capacity)
    asked = lax.all_to_all(packed, "dp", split_axis=0, concat_axis=0, tiled=True)

    for_partner = project(visual_tokens, weight_half, 1 - tensor, True)
    from_partner = lax.ppermute(for_partner, "tensor", [(0, 1), (1, 0)])
    own = project(visual_tokens, weight_half, tensor, False)

    cached, cached_log = cached_attention(
        step_queries, cache_keys, cache_values, step_keys, step_values, cache_lengths
    )

    device = lax.axis_index("dp")
    own_lengths = lax.dynamic_index_in_dim(image_lengths, device, 0, keepdims=False)
    own_device = (
        lax.dynamic_slice_in_dim(image_owner, device * images_local, images_local) // rows_local
    )
    order = jnp.arange(images_local)
    earlier = order[None, :] < order[:, None]
    own_rank = jnp.sum(
        ((own_device[:, None] == own_device[None, :]) & earlier).astype(jnp.int32), axis=1
    )
    starts = jnp.sum(jnp.where(earlier, own_lengths[None, :], 0), axis=1)
    window_at = jnp.minimum(starts // 16 * 16, visual_tokens.shape[0] - VMAX - 16)
    places = jnp.stack([own_device * capacity + own_rank, window_at, starts - window_at, own_lengths])

    split = 2 * width_local
    squares = for_partner[:, split : split + 1] + from_partner[:, split : split + 1]
    pairs = (own + from_partner[:, :split]) * lax.rsqrt(squares / D + EPSILON)
    pairs = pairs.astype(jnp.bfloat16)

    answers = visual_attention(places, asked, pairs)
    returned = lax.all_to_all(answers, "dp", split_axis=0, concat_axis=0, tiled=True)
    return merge(slot_of_row, returned, cached, cached_log)


def solution(mesh):
    return jax.shard_map(
        shards,
        mesh=mesh,
        in_specs=(
            P(("groups", "dp"), "tensor"),
            P("tensor", None, None, None),
            P("groups", None),
            P("groups"),
            P(("groups", "dp")),
            P(("groups", "dp"), None, "tensor"),
            P(("groups", "dp"), None, "tensor"),
            P(("groups", "dp"), None, "tensor"),
            P(("groups", "dp"), None, "tensor"),
            P(("groups", "dp"), None, "tensor"),
        ),
        out_specs=P(("groups", "dp"), None, "tensor"),
        check_vma=False,
    )
```

```python
import jax
import jax.numpy as jnp
from jax import lax
from jax.experimental import pallas as pl
from jax.experimental.pallas import tpu as pltpu
from jax.sharding import PartitionSpec as P

D = 8192
HD = 128
STEPS = 4
VMAX = 48
EPSILON = 1e-06
LANES = 128
FLOOR = -1e30
PIECES = 4
FAR_BYTES = 40 << 20


def dot_t(a, b):
    return lax.dot_general(a, b, (((1,), (1,)), ((), ())), preferred_element_type=jnp.float32)


def dot(a, b):
    return jnp.dot(a, b, preferred_element_type=jnp.float32)


def pack_queries(image_owner, step_queries, devices, capacity):
    rows = step_queries.shape[0]
    images = image_owner.shape[0] // devices
    slots = devices * capacity

    def kernel(owner_hbm, query_hbm, packed, slot_of_row, owner, queries, row_of_slot, in_sems, sems):
        read_owner = pltpu.make_async_copy(owner_hbm, owner, in_sems.at[0])
        read_queries = pltpu.make_async_copy(query_hbm, queries, in_sems.at[1])
        read_owner.start()
        read_queries.start()
        base = lax.axis_index("dp") * rows
        for r in range(rows):
            slot_of_row[r] = -1
        for slot in range(slots):
            row_of_slot[slot] = 0
        read_owner.wait()
        copies = []
        for s in range(devices):
            rank = jnp.int32(0)
            for i in range(images):
                row = owner[s * images + i] - base
                local = jnp.logical_and(row >= 0, row < rows)
                slot = s * capacity + rank
                row_of_slot[jnp.where(local, slot, slots)] = row
                slot_of_row[jnp.where(local, row, rows)] = slot
                rank = rank + local.astype(jnp.int32)
            if s == 0:
                read_queries.wait()
            for k in range(capacity):
                slot = s * capacity + k
                copy = pltpu.make_async_copy(
                    queries.at[row_of_slot[slot]], packed.at[slot], sems.at[slot]
                )
                copy.start()
                copies.append(copy)
        for copy in copies:
            copy.wait()

    return pl.pallas_call(
        kernel,
        in_specs=[pl.BlockSpec(memory_space=pl.ANY), pl.BlockSpec(memory_space=pl.ANY)],
        out_specs=[pl.BlockSpec(memory_space=pl.ANY), pl.BlockSpec(memory_space=pltpu.SMEM)],
        out_shape=[
            jax.ShapeDtypeStruct((slots,) + step_queries.shape[1:], step_queries.dtype),
            jax.ShapeDtypeStruct((rows + 1,), jnp.int32),
        ],
        scratch_shapes=[
            pltpu.SMEM(image_owner.shape, jnp.int32),
            pltpu.VMEM(step_queries.shape, step_queries.dtype),
            pltpu.SMEM((slots + 1,), jnp.int32),
            pltpu.SemaphoreType.DMA((2,)),
            pltpu.SemaphoreType.DMA((slots,)),
        ],
        name="pack_queries",
    )(image_owner, step_queries)


def project(tokens, weight):
    count, depth = tokens.shape
    width = weight.shape[2] // 2
    columns = 2 * width + LANES
    piece = count // PIECES
    sizes = [512, 512] + [1024] * ((depth - 1024) // 1024)
    starts = [sum(sizes[:c]) for c in range(len(sizes))]
    chunks = len(sizes)
    ahead = 3

    def kernel(token_hbm, weight_hbm, *refs):
        pieces = refs[:PIECES]
        ours_hbm, theirs_s, ours_s, token_s, weight_s, sems, out_sems = refs[PIECES:]
        mine = lax.axis_index("tensor")

        def lanes(half):
            return pl.ds(pl.multiple_of(half * width, width), width)

        def product(x, w):
            w = jnp.swapaxes(w, 0, 1)
            return dot(x, jnp.concatenate([w[0], w[1]], axis=1))

        loads = []
        for c in range(chunks):
            span = pl.ds(starts[c], sizes[c])
            loads.append(
                [
                    pltpu.make_async_copy(
                        token_hbm.at[:, span], token_s.at[:, span], sems.at[0, c]
                    ),
                    pltpu.make_async_copy(
                        weight_hbm.at[span, :, lanes(1 - mine)],
                        weight_s.at[0, span],
                        sems.at[1, c],
                    ),
                ]
            )
        loads.append(
            [pltpu.make_async_copy(weight_hbm.at[:, :, lanes(mine)], weight_s.at[1], sems.at[2, 0])]
        )

        def start(c):
            if c < len(loads):
                for load in loads[c]:
                    load.start()

        for c in range(ahead):
            start(c)
        squares = jnp.zeros((count, LANES), jnp.float32)
        for c in range(chunks):
            for load in loads[c]:
                load.wait()
            start(c + ahead)
            span = slice(starts[c], starts[c] + sizes[c])
            x = token_s[:, span]
            part = product(x, weight_s[0, span])
            if c == 0:
                theirs_s[:, : 2 * width] = part
            else:
                theirs_s[:, : 2 * width] += part
            for lane in range(0, sizes[c], LANES):
                wide = x[:, lane : lane + LANES].astype(jnp.float32)
                squares += wide * wide
        squares = jnp.broadcast_to(jnp.sum(squares, axis=1, keepdims=True), (count, LANES))
        theirs_s[:, 2 * width :] = squares
        stores = []
        for k in range(PIECES):
            store = pltpu.make_async_copy(
                theirs_s.at[pl.ds(k * piece, piece)], pieces[k], out_sems.at[k]
            )
            store.start()
            stores.append(store)
        ours_s[:, 2 * width :] = squares
        for load in loads[chunks]:
            load.wait()
        ours_s[:, : 2 * width] = product(token_s[...], weight_s[1])
        store = pltpu.make_async_copy(
            ours_s, ours_hbm.at[pl.ds(0, count)], out_sems.at[PIECES]
        )
        store.start()
        stores.append(store)
        for store in stores:
            store.wait()

    hbm = pl.BlockSpec(memory_space=pltpu.HBM)
    *theirs, ours = pl.pallas_call(
        kernel,
        in_specs=[hbm, hbm],
        out_specs=[pl.BlockSpec(memory_space=pl.ANY)] * (PIECES + 1),
        out_shape=[jax.ShapeDtypeStruct((piece, columns), jnp.float32)] * PIECES
        + [jax.ShapeDtypeStruct((FAR_BYTES // (4 * columns), columns), jnp.float32)],
        scratch_shapes=[
            pltpu.VMEM((count, columns), jnp.float32),
            pltpu.VMEM((count, columns), jnp.float32),
            pltpu.VMEM(tokens.shape, tokens.dtype),
            pltpu.VMEM((2, depth, 2, width), weight.dtype),
            pltpu.SemaphoreType.DMA((3, chunks)),
            pltpu.SemaphoreType.DMA((PIECES + 1,)),
        ],
        compiler_params=pltpu.CompilerParams(vmem_limit_bytes=60 << 20),
        cost_estimate=pl.CostEstimate(flops=1 << 20, bytes_accessed=1 << 16, transcendentals=0),
        name="project",
    )(tokens, weight)
    return theirs, ours


def cached_attention(queries, cache_keys, cache_values, step_keys, step_values, lengths):
    rows, context, width = cache_keys.shape
    kv_local = width // HD
    heads = queries.shape[2] // HD
    group = heads // kv_local
    stacked = group * STEPS
    block = 8 if rows % 8 == 0 else 2
    scale = HD**-0.5

    def kernel(length_ref, q_ref, k_ref, v_ref, sk_ref, sv_ref, out_ref, q_s, sk_s, sv_s):
        first = pl.program_id(0) * block
        for r in range(block):
            for g in range(kv_local):
                sk_s[g, r * STEPS : (r + 1) * STEPS, :] = sk_ref[
                    r, :, g * HD : (g + 1) * HD
                ].astype(jnp.float32)
                sv_s[g, r * STEPS : (r + 1) * STEPS, :] = sv_ref[
                    r, :, g * HD : (g + 1) * HD
                ].astype(jnp.float32)
                for j in range(group):
                    h = g * group + j
                    at = r * stacked + j * STEPS
                    q_s[g, at : at + STEPS, :] = q_ref[r, :, h * HD : (h + 1) * HD].astype(
                        jnp.float32
                    )
        lane = lax.broadcasted_iota(jnp.int32, (STEPS, LANES), 1)
        logs = [jnp.zeros((STEPS, LANES), jnp.float32) for _ in range(block)]
        for g in range(kv_local):
            q = q_s[g].astype(jnp.bfloat16)
            steps = dot_t(q, sk_s[g].astype(jnp.bfloat16)) * scale
            at_row = lax.broadcasted_iota(jnp.int32, steps.shape, 0)
            at_key = lax.broadcasted_iota(jnp.int32, steps.shape, 1)
            own = (at_row // stacked == at_key // STEPS) & (at_key % STEPS <= at_row % STEPS)
            steps = jnp.where(own, steps, FLOOR)
            step_peak = jnp.max(steps, axis=1, keepdims=True)
            scores = []
            position = lax.broadcasted_iota(jnp.int32, (stacked, context), 1)
            for r in range(block):
                part = dot_t(q[r * stacked : (r + 1) * stacked], k_ref[r, :, g * HD : (g + 1) * HD])
                scores.append(jnp.where(position < length_ref[first + r], part * scale, FLOOR))
            cached = jnp.concatenate(scores, axis=0)
            peak = jnp.maximum(jnp.max(cached, axis=1, keepdims=True), step_peak)
            cached = jnp.exp(cached - peak)
            steps = jnp.where(own, jnp.exp(steps - peak), 0.0)
            total = jnp.sum(cached, axis=1, keepdims=True) + jnp.sum(steps, axis=1, keepdims=True)
            cached = cached.astype(jnp.bfloat16)
            mixed = dot(steps.astype(jnp.bfloat16), sv_s[g].astype(jnp.bfloat16))
            inverse = 1.0 / total
            log = jnp.broadcast_to(peak + jnp.log(total), (block * stacked, LANES))
            for r in range(block):
                span = slice(r * stacked, (r + 1) * stacked)
                part = dot(cached[span], v_ref[r, :, g * HD : (g + 1) * HD])
                part = (part + mixed[span]) * inverse[span]
                for j in range(group):
                    h = g * group + j
                    head = slice(j * STEPS, (j + 1) * STEPS)
                    out_ref[r, :, h * HD : (h + 1) * HD] = part[head]
                    at = r * stacked + j * STEPS
                    logs[r] = jnp.where(lane == h, log[at : at + STEPS], logs[r])
        for r in range(block):
            out_ref[r, :, heads * HD :] = logs[r]

    def spec(array):
        return pl.BlockSpec((block,) + array.shape[1:], lambda i, length_ref: (i, 0, 0))

    return pl.pallas_call(
        kernel,
        grid_spec=pltpu.PrefetchScalarGridSpec(
            num_scalar_prefetch=1,
            grid=(rows // block,),
            in_specs=[
                spec(queries),
                spec(cache_keys),
                spec(cache_values),
                spec(step_keys),
                spec(step_values),
            ],
            out_specs=pl.BlockSpec(
                (block, STEPS, heads * HD + LANES), lambda i, length_ref: (i, 0, 0)
            ),
            scratch_shapes=[
                pltpu.VMEM((kv_local, block * stacked, HD), jnp.float32),
                pltpu.VMEM((kv_local, block * STEPS, HD), jnp.float32),
                pltpu.VMEM((kv_local, block * STEPS, HD), jnp.float32),
            ],
        ),
        out_shape=jax.ShapeDtypeStruct(
            (FAR_BYTES // (4 * STEPS * (heads * HD + LANES)), STEPS, heads * HD + LANES), jnp.float32
        ),
        compiler_params=pltpu.CompilerParams(vmem_limit_bytes=60 << 20),
        cost_estimate=pl.CostEstimate(flops=1 << 20, bytes_accessed=1 << 16, transcendentals=0),
        name="cached_attention",
    )(lengths, queries, cache_keys, cache_values, step_keys, step_values)


def visual_attention(places, queries, ours, received):
    images = places.shape[1]
    slots, _, full = queries.shape
    heads = full // HD
    columns = ours.shape[1]
    split = columns - LANES
    kv_local = split // (2 * HD)
    piece = received[0].shape[0]
    count = piece * PIECES
    group = heads // kv_local
    stacked = group * STEPS
    window = VMAX + 16
    scale = HD**-0.5

    def kernel(place_ref, q_ref, ours_hbm, *refs):
        received_hbm = refs[:PIECES]
        out_hbm, ours_s, received_s, pair_ref, q_s, score_s, weight_s, out_ref, load_sems, sems = refs[
            PIECES:
        ]
        loads = []
        for k in range(PIECES):
            rows = pl.ds(k * piece, piece)
            pair = (
                pltpu.make_async_copy(ours_hbm.at[rows], ours_s.at[rows], load_sems.at[0, k]),
                pltpu.make_async_copy(received_hbm[k], received_s.at[rows], load_sems.at[1, k]),
            )
            for load in pair:
                load.start()
            loads.append(pair)
        stores = []
        for i in range(images):
            slot = place_ref[0, i]
            for h in range(heads):
                q_s[i, h * STEPS : (h + 1) * STEPS, :] = q_ref[
                    slot, :, h * HD : (h + 1) * HD
                ].astype(jnp.float32)
        for k in range(PIECES):
            for load in loads[k]:
                load.wait()
            rows = slice(k * piece, (k + 1) * piece)
            factor = lax.rsqrt((ours_s[rows, split:] + received_s[rows, split:]) / D + EPSILON)
            for at in range(0, split, LANES):
                lanes = slice(at, at + LANES)
                total = (ours_s[rows, lanes] + received_s[rows, lanes]) * factor
                pair_ref[rows, lanes] = total.astype(pair_ref.dtype)
        for i in range(images):
            rows = pl.ds(pl.multiple_of(place_ref[1, i], 16), window)
            q = q_s[i].astype(jnp.bfloat16)
            for g in range(kv_local):
                score_s[i, g * stacked : (g + 1) * stacked, :] = dot_t(
                    q[g * stacked : (g + 1) * stacked], pair_ref[rows, g * HD : (g + 1) * HD]
                )
        column = lax.broadcasted_iota(jnp.int32, (heads * STEPS, window), 1)
        inverses = []
        logs = []
        for i in range(images):
            start = place_ref[2, i]
            live = (column >= start) & (column < start + place_ref[3, i])
            scores = jnp.where(live, score_s[i] * scale, FLOOR)
            peak = jnp.max(scores, axis=1, keepdims=True)
            weights = jnp.exp(scores - peak)
            total = jnp.sum(weights, axis=1, keepdims=True)
            weight_s[i] = weights.astype(jnp.bfloat16)
            inverses.append(1.0 / total)
            logs.append(jnp.broadcast_to(peak + jnp.log(total), (heads * STEPS, LANES)))
        lane = lax.broadcasted_iota(jnp.int32, (STEPS, LANES), 1)
        for i in range(images):
            rows = pl.ds(pl.multiple_of(place_ref[1, i], 16), window)
            for g in range(kv_local):
                at = (kv_local + g) * HD
                part = dot(
                    weight_s[i, g * stacked : (g + 1) * stacked, :], pair_ref[rows, at : at + HD]
                )
                part = part * inverses[i][g * stacked : (g + 1) * stacked]
                for j in range(group):
                    h = g * group + j
                    out_ref[i, :, h * HD : (h + 1) * HD] = part[
                        j * STEPS : (j + 1) * STEPS
                    ].astype(out_ref.dtype)
            packed = jnp.zeros((STEPS, LANES), jnp.float32)
            for h in range(heads):
                log = logs[i][h * STEPS : (h + 1) * STEPS]
                packed = jnp.where(lane % heads == h, log, packed)
            first = packed.astype(jnp.bfloat16).astype(jnp.float32)
            rest = packed - first
            second = rest.astype(jnp.bfloat16).astype(jnp.float32)
            third = rest - second
            out_ref[i, :, full:] = jnp.where(
                lane < heads,
                first,
                jnp.where(lane < 2 * heads, second, jnp.where(lane < 3 * heads, third, 0.0)),
            ).astype(out_ref.dtype)
            store = pltpu.make_async_copy(out_ref.at[i], out_hbm.at[place_ref[0, i]], sems.at[i])
            store.start()
            stores.append(store)
        for store in stores:
            store.wait()

    anywhere = pl.BlockSpec(memory_space=pl.ANY)
    return pl.pallas_call(
        kernel,
        in_specs=[
            pl.BlockSpec(memory_space=pltpu.SMEM),
            pl.BlockSpec(memory_space=pltpu.VMEM),
        ]
        + [anywhere] * (1 + PIECES),
        out_specs=anywhere,
        out_shape=jax.ShapeDtypeStruct((slots, STEPS, full + LANES), queries.dtype),
        scratch_shapes=[
            pltpu.VMEM((count, columns), jnp.float32),
            pltpu.VMEM((count, columns), jnp.float32),
            pltpu.VMEM((count, split), jnp.bfloat16),
            pltpu.VMEM((images, heads * STEPS, HD), jnp.float32),
            pltpu.VMEM((images, heads * STEPS, window), jnp.float32),
            pltpu.VMEM((images, heads * STEPS, window), jnp.bfloat16),
            pltpu.VMEM((images, STEPS, full + LANES), queries.dtype),
            pltpu.SemaphoreType.DMA((2, PIECES)),
            pltpu.SemaphoreType.DMA((images,)),
        ],
        compiler_params=pltpu.CompilerParams(vmem_limit_bytes=32 << 20),
        name="visual_attention",
    )(places, queries, ours, *received)


def merge(slot_of_row, returned, cached, rows):
    full = cached.shape[2] - LANES
    heads = full // HD
    runs = 3 if rows % 3 == 0 else 1
    run = rows // runs

    def kernel(slot_ref, returned_ref, cached_hbm, out_hbm, cached_s, out_s, sems):
        loads = []
        stores = []
        for k in range(runs):
            span = pl.ds(k * run, run)
            load = pltpu.make_async_copy(cached_hbm.at[span], cached_s.at[span], sems.at[0, k])
            load.start()
            loads.append(load)
        for k in range(runs):
            loads[k].wait()
            for r in range(k * run, (k + 1) * run):
                present = slot_ref[r] >= 0
                slot = jnp.maximum(slot_ref[r], 0)
                terms = returned_ref[slot, :, full:].astype(jnp.float32)
                log = (
                    terms[:, :heads] + terms[:, heads : 2 * heads] + terms[:, 2 * heads : 3 * heads]
                )
                share = 1.0 / (1.0 + jnp.exp(cached_s[r, :, full : full + heads] - log))
                for h in range(heads):
                    lanes = slice(h * HD, (h + 1) * HD)
                    own = cached_s[r, :, lanes]
                    other = returned_ref[slot, :, lanes].astype(jnp.float32)
                    mixed = own + share[:, h : h + 1] * (other - own)
                    out_s[r, :, lanes] = jnp.where(present, mixed, own).astype(out_s.dtype)
            span = pl.ds(k * run, run)
            store = pltpu.make_async_copy(out_s.at[span], out_hbm.at[span], sems.at[1, k])
            store.start()
            stores.append(store)
        for store in stores:
            store.wait()

    anywhere = pl.BlockSpec(memory_space=pl.ANY)
    return pl.pallas_call(
        kernel,
        in_specs=[
            pl.BlockSpec(memory_space=pltpu.SMEM),
            pl.BlockSpec(memory_space=pltpu.VMEM),
            anywhere,
        ],
        out_specs=anywhere,
        out_shape=jax.ShapeDtypeStruct((rows, STEPS, full), jnp.bfloat16),
        scratch_shapes=[
            pltpu.VMEM((rows, STEPS, full + LANES), jnp.float32),
            pltpu.VMEM((rows, STEPS, full), jnp.bfloat16),
            pltpu.SemaphoreType.DMA((2, runs)),
        ],
        compiler_params=pltpu.CompilerParams(vmem_limit_bytes=32 << 20),
        name="merge",
    )(slot_of_row, returned, cached)


def shards(
    visual_tokens,
    kv_weight,
    image_lengths,
    image_owner,
    cache_lengths,
    cache_keys,
    cache_values,
    step_queries,
    step_keys,
    step_values,
):
    devices = lax.axis_size("dp")
    rows_local = cache_lengths.shape[0]
    images_local = image_lengths.shape[1]
    capacity = -(-rows_local // devices)
    weight_half = kv_weight[0]
    packed, slot_of_row = pack_queries(image_owner, step_queries, devices, capacity)
    tokens, packed = lax.optimization_barrier((visual_tokens, packed))
    asked = lax.all_to_all(packed, "dp", split_axis=0, concat_axis=0, tiled=True)
    for_partner, ours = project(tokens, weight_half)
    from_partner = [lax.ppermute(piece, "tensor", [(0, 1), (1, 0)]) for piece in for_partner]

    cached = cached_attention(
        step_queries, cache_keys, cache_values, step_keys, step_values, cache_lengths
    )

    device = lax.axis_index("dp")
    own_lengths = lax.dynamic_index_in_dim(image_lengths, device, 0, keepdims=False)
    own_device = (
        lax.dynamic_slice_in_dim(image_owner, device * images_local, images_local) // rows_local
    )
    order = jnp.arange(images_local)
    earlier = order[None, :] < order[:, None]
    own_rank = jnp.sum(
        ((own_device[:, None] == own_device[None, :]) & earlier).astype(jnp.int32), axis=1
    )
    starts = jnp.sum(jnp.where(earlier, own_lengths[None, :], 0), axis=1)
    window_at = jnp.minimum(starts // 16 * 16, visual_tokens.shape[0] - VMAX - 16)
    places = jnp.stack([own_device * capacity + own_rank, window_at, starts - window_at, own_lengths])

    answers = visual_attention(places, asked, ours, from_partner)
    returned = lax.all_to_all(answers, "dp", split_axis=0, concat_axis=0, tiled=True)
    return merge(slot_of_row, returned, cached, rows_local)


def solution(mesh):
    return jax.shard_map(
        shards,
        mesh=mesh,
        in_specs=(
            P(("groups", "dp"), "tensor"),
            P("tensor", None, None, None),
            P("groups", None),
            P("groups"),
            P(("groups", "dp")),
            P(("groups", "dp"), None, "tensor"),
            P(("groups", "dp"), None, "tensor"),
            P(("groups", "dp"), None, "tensor"),
            P(("groups", "dp"), None, "tensor"),
            P(("groups", "dp"), None, "tensor"),
        ),
        out_specs=P(("groups", "dp"), None, "tensor"),
        check_vma=False,
    )
```

```python
import jax
import jax.numpy as jnp
from jax import lax
from jax.experimental import pallas as pl
from jax.experimental.pallas import tpu as pltpu
from jax.sharding import PartitionSpec as P

D = 8192
HD = 128
STEPS = 4
VMAX = 48
EPSILON = 1e-06
LANES = 128
FLOOR = -1e30
PIECES = 2
FAR_BYTES = 40 << 20


def dot_t(a, b):
    return lax.dot_general(a, b, (((1,), (1,)), ((), ())), preferred_element_type=jnp.float32)


def dot(a, b):
    return jnp.dot(a, b, preferred_element_type=jnp.float32)


def three_terms(value, lane, step):
    first = value.astype(jnp.bfloat16).astype(jnp.float32)
    rest = value - first
    second = rest.astype(jnp.bfloat16).astype(jnp.float32)
    third = jnp.where(lane < 3 * step, rest - second, 0.0)
    terms = jnp.where(lane < step, first, jnp.where(lane < 2 * step, second, third))
    return terms.astype(jnp.bfloat16)


def pack_queries(image_owner, step_queries, devices, capacity):
    rows = step_queries.shape[0]
    images = image_owner.shape[0] // devices
    slots = devices * capacity
    table = (rows // LANES + 1) * LANES

    def kernel(
        owner_hbm, query_hbm, packed, slot_out, owner, queries, row_of_slot, slot_of_row, in_sems, sems
    ):
        read_owner = pltpu.make_async_copy(owner_hbm, owner, in_sems.at[0])
        read_queries = pltpu.make_async_copy(query_hbm, queries, in_sems.at[1])
        read_owner.start()
        read_queries.start()
        base = lax.axis_index("dp") * rows
        for r in range(rows):
            slot_of_row[r] = -1
        for slot in range(slots):
            row_of_slot[slot] = 0
        read_owner.wait()
        copies = []
        for s in range(devices):
            rank = jnp.int32(0)
            for i in range(images):
                row = owner[s * images + i] - base
                local = jnp.logical_and(row >= 0, row < rows)
                slot = s * capacity + rank
                row_of_slot[jnp.where(local, slot, slots)] = row
                slot_of_row[jnp.where(local, row, rows)] = slot
                rank = rank + local.astype(jnp.int32)
            if s == 0:
                read_queries.wait()
            for k in range(capacity):
                slot = s * capacity + k
                copy = pltpu.make_async_copy(
                    queries.at[row_of_slot[slot]], packed.at[slot], sems.at[slot]
                )
                copy.start()
                copies.append(copy)
        write_slots = pltpu.make_async_copy(slot_of_row, slot_out, in_sems.at[2])
        write_slots.start()
        for copy in copies:
            copy.wait()
        write_slots.wait()

    return pl.pallas_call(
        kernel,
        in_specs=[pl.BlockSpec(memory_space=pl.ANY), pl.BlockSpec(memory_space=pl.ANY)],
        out_specs=[pl.BlockSpec(memory_space=pl.ANY), pl.BlockSpec(memory_space=pl.ANY)],
        out_shape=[
            jax.ShapeDtypeStruct((slots,) + step_queries.shape[1:], step_queries.dtype),
            jax.ShapeDtypeStruct((table,), jnp.int32),
        ],
        scratch_shapes=[
            pltpu.SMEM(image_owner.shape, jnp.int32),
            pltpu.VMEM(step_queries.shape, step_queries.dtype),
            pltpu.SMEM((slots + 1,), jnp.int32),
            pltpu.SMEM((table,), jnp.int32),
            pltpu.SemaphoreType.DMA((3,)),
            pltpu.SemaphoreType.DMA((slots,)),
        ],
        name="pack_queries",
    )(image_owner, step_queries)


def project(tokens, weight):
    count, depth = tokens.shape
    width = weight.shape[2] // 2
    columns = 2 * width + LANES
    piece = count // PIECES
    sizes = [512, 512] + [1024] * ((depth - 1024) // 1024)
    starts = [sum(sizes[:c]) for c in range(len(sizes))]
    chunks = len(sizes)
    ahead = 3

    def kernel(token_hbm, weight_hbm, *refs):
        pieces = refs[:PIECES]
        ours_hbm, ours_s, token_s, weight_s, sems, out_sem = refs[PIECES:]
        mine = lax.axis_index("tensor")

        def lanes(half):
            return pl.ds(pl.multiple_of(half * width, width), width)

        def product(x, w):
            w = jnp.swapaxes(w, 0, 1)
            return dot(x, jnp.concatenate([w[0], w[1]], axis=1))

        loads = []
        for c in range(chunks):
            span = pl.ds(starts[c], sizes[c])
            loads.append(
                [
                    pltpu.make_async_copy(
                        token_hbm.at[:, span], token_s.at[:, span], sems.at[0, c]
                    ),
                    pltpu.make_async_copy(
                        weight_hbm.at[span, :, lanes(mine)], weight_s.at[0, span], sems.at[1, c]
                    ),
                ]
            )
        loads.append(
            [
                pltpu.make_async_copy(
                    weight_hbm.at[:, :, lanes(1 - mine)], weight_s.at[1], sems.at[2, 0]
                )
            ]
        )

        def start(c):
            if c < len(loads):
                for load in loads[c]:
                    load.start()

        for c in range(ahead):
            start(c)
        squares = jnp.zeros((count, LANES), jnp.float32)
        for c in range(chunks):
            for load in loads[c]:
                load.wait()
            start(c + ahead)
            span = slice(starts[c], starts[c] + sizes[c])
            x = token_s[:, span]
            part = product(x, weight_s[0, span])
            if c == 0:
                ours_s[:, : 2 * width] = part
            else:
                ours_s[:, : 2 * width] += part
            for lane in range(0, sizes[c], LANES):
                wide = x[:, lane : lane + LANES].astype(jnp.float32)
                squares += wide * wide
        squares = jnp.broadcast_to(jnp.sum(squares, axis=1, keepdims=True), (count, LANES))
        ours_s[:, 2 * width :] = squares
        store = pltpu.make_async_copy(ours_s, ours_hbm.at[pl.ds(0, count)], out_sem)
        store.start()
        terms = three_terms(squares, lax.broadcasted_iota(jnp.int32, (count, LANES), 1), 1)
        for load in loads[chunks]:
            load.wait()
        theirs = product(token_s[...], weight_s[1]).astype(jnp.bfloat16)
        for k, piece_ref in enumerate(pieces):
            span = slice(k * piece, (k + 1) * piece)
            piece_ref[:, : 2 * width] = theirs[span]
            piece_ref[:, 2 * width :] = terms[span]
        store.wait()

    hbm = pl.BlockSpec(memory_space=pltpu.HBM)
    *theirs, ours = pl.pallas_call(
        kernel,
        in_specs=[hbm, hbm],
        out_specs=[pl.BlockSpec(memory_space=pltpu.VMEM)] * PIECES
        + [pl.BlockSpec(memory_space=pl.ANY)],
        out_shape=[jax.ShapeDtypeStruct((piece, columns), jnp.bfloat16)] * PIECES
        + [jax.ShapeDtypeStruct((FAR_BYTES // (4 * columns), columns), jnp.float32)],
        scratch_shapes=[
            pltpu.VMEM((count, columns), jnp.float32),
            pltpu.VMEM(tokens.shape, tokens.dtype),
            pltpu.VMEM((2, depth, 2, width), weight.dtype),
            pltpu.SemaphoreType.DMA((3, chunks)),
            pltpu.SemaphoreType.DMA,
        ],
        compiler_params=pltpu.CompilerParams(vmem_limit_bytes=60 << 20),
        cost_estimate=pl.CostEstimate(flops=1 << 20, bytes_accessed=1 << 16, transcendentals=0),
        name="project",
    )(tokens, weight)
    return theirs, ours


def cached_attention(queries, cache_keys, cache_values, step_keys, step_values, lengths):
    rows, context, width = cache_keys.shape
    kv_local = width // HD
    heads = queries.shape[2] // HD
    group = heads // kv_local
    stacked = group * STEPS
    block = 8 if rows % 8 == 0 else 2
    scale = HD**-0.5

    def kernel(length_ref, q_ref, k_ref, v_ref, sk_ref, sv_ref, out_ref, q_s, sk_s, sv_s):
        first = pl.program_id(0) * block
        for r in range(block):
            for g in range(kv_local):
                sk_s[g, r * STEPS : (r + 1) * STEPS, :] = sk_ref[
                    r, :, g * HD : (g + 1) * HD
                ].astype(jnp.float32)
                sv_s[g, r * STEPS : (r + 1) * STEPS, :] = sv_ref[
                    r, :, g * HD : (g + 1) * HD
                ].astype(jnp.float32)
                for j in range(group):
                    h = g * group + j
                    at = r * stacked + j * STEPS
                    q_s[g, at : at + STEPS, :] = q_ref[r, :, h * HD : (h + 1) * HD].astype(
                        jnp.float32
                    )
        lane = lax.broadcasted_iota(jnp.int32, (STEPS, LANES), 1)
        logs = [jnp.zeros((STEPS, LANES), jnp.float32) for _ in range(block)]
        for g in range(kv_local):
            q = q_s[g].astype(jnp.bfloat16)
            steps = dot_t(q, sk_s[g].astype(jnp.bfloat16)) * scale
            at_row = lax.broadcasted_iota(jnp.int32, steps.shape, 0)
            at_key = lax.broadcasted_iota(jnp.int32, steps.shape, 1)
            own = (at_row // stacked == at_key // STEPS) & (at_key % STEPS <= at_row % STEPS)
            steps = jnp.where(own, steps, FLOOR)
            step_peak = jnp.max(steps, axis=1, keepdims=True)
            scores = []
            position = lax.broadcasted_iota(jnp.int32, (stacked, context), 1)
            for r in range(block):
                part = dot_t(q[r * stacked : (r + 1) * stacked], k_ref[r, :, g * HD : (g + 1) * HD])
                scores.append(jnp.where(position < length_ref[first + r], part * scale, FLOOR))
            cached = jnp.concatenate(scores, axis=0)
            peak = jnp.maximum(jnp.max(cached, axis=1, keepdims=True), step_peak)
            cached = jnp.exp(cached - peak)
            steps = jnp.where(own, jnp.exp(steps - peak), 0.0)
            total = jnp.sum(cached, axis=1, keepdims=True) + jnp.sum(steps, axis=1, keepdims=True)
            cached = cached.astype(jnp.bfloat16)
            mixed = dot(steps.astype(jnp.bfloat16), sv_s[g].astype(jnp.bfloat16))
            inverse = 1.0 / total
            log = jnp.broadcast_to(peak + jnp.log(total), (block * stacked, LANES))
            for r in range(block):
                span = slice(r * stacked, (r + 1) * stacked)
                part = dot(cached[span], v_ref[r, :, g * HD : (g + 1) * HD])
                part = (part + mixed[span]) * inverse[span]
                for j in range(group):
                    h = g * group + j
                    head = slice(j * STEPS, (j + 1) * STEPS)
                    out_ref[r, :, h * HD : (h + 1) * HD] = part[head]
                    at = r * stacked + j * STEPS
                    logs[r] = jnp.where(lane == h, log[at : at + STEPS], logs[r])
        for r in range(block):
            out_ref[r, :, heads * HD :] = logs[r]

    def spec(array):
        return pl.BlockSpec((block,) + array.shape[1:], lambda i, length_ref: (i, 0, 0))

    return pl.pallas_call(
        kernel,
        grid_spec=pltpu.PrefetchScalarGridSpec(
            num_scalar_prefetch=1,
            grid=(rows // block,),
            in_specs=[
                spec(queries),
                spec(cache_keys),
                spec(cache_values),
                spec(step_keys),
                spec(step_values),
            ],
            out_specs=pl.BlockSpec(
                (block, STEPS, heads * HD + LANES), lambda i, length_ref: (i, 0, 0)
            ),
            scratch_shapes=[
                pltpu.VMEM((kv_local, block * stacked, HD), jnp.float32),
                pltpu.VMEM((kv_local, block * STEPS, HD), jnp.float32),
                pltpu.VMEM((kv_local, block * STEPS, HD), jnp.float32),
            ],
        ),
        out_shape=jax.ShapeDtypeStruct(
            (FAR_BYTES // (4 * STEPS * (heads * HD + LANES)), STEPS, heads * HD + LANES), jnp.float32
        ),
        compiler_params=pltpu.CompilerParams(vmem_limit_bytes=60 << 20),
        cost_estimate=pl.CostEstimate(flops=1 << 20, bytes_accessed=1 << 16, transcendentals=0),
        name="cached_attention",
    )(lengths, queries, cache_keys, cache_values, step_keys, step_values)


def visual_attention(places, queries, ours, received):
    images = places.shape[0] // 4
    slots, _, full = queries.shape
    heads = full // HD
    columns = ours.shape[1]
    split = columns - LANES
    kv_local = split // (2 * HD)
    piece = received[0].shape[0]
    count = piece * PIECES
    group = heads // kv_local
    stacked = group * STEPS
    window = VMAX + 16
    scale = HD**-0.5

    def kernel(place_hbm, q_ref, ours_hbm, *refs):
        received_hbm = refs[:PIECES]
        out_hbm, place_ref, ours_s, received_s, pair_ref, q_s, score_s, weight_s, out_ref = refs[
            PIECES:-3
        ]
        place_sem, load_sems, sems = refs[-3:]
        read_places = pltpu.make_async_copy(place_hbm, place_ref, place_sem)
        read_places.start()
        loads = []
        for k in range(PIECES):
            rows = pl.ds(k * piece, piece)
            pair = (
                pltpu.make_async_copy(ours_hbm.at[rows], ours_s.at[rows], load_sems.at[0, k]),
                pltpu.make_async_copy(received_hbm[k], received_s.at[rows], load_sems.at[1, k]),
            )
            for load in pair:
                load.start()
            loads.append(pair)
        stores = []
        read_places.wait()
        for i in range(images):
            slot = place_ref[0 * images + i]
            for h in range(heads):
                q_s[i, h * STEPS : (h + 1) * STEPS, :] = q_ref[
                    slot, :, h * HD : (h + 1) * HD
                ].astype(jnp.float32)
        for k in range(PIECES):
            for load in loads[k]:
                load.wait()
            rows = slice(k * piece, (k + 1) * piece)
            squares = jnp.sum(
                received_s[rows, split:].astype(jnp.float32), axis=1, keepdims=True
            )
            factor = lax.rsqrt((ours_s[rows, split:] + squares) / D + EPSILON)
            for at in range(0, split, LANES):
                lanes = slice(at, at + LANES)
                total = (ours_s[rows, lanes] + received_s[rows, lanes].astype(jnp.float32)) * factor
                pair_ref[rows, lanes] = total.astype(pair_ref.dtype)
        for i in range(images):
            rows = pl.ds(pl.multiple_of(place_ref[1 * images + i], 16), window)
            q = q_s[i].astype(jnp.bfloat16)
            for g in range(kv_local):
                score_s[i, g * stacked : (g + 1) * stacked, :] = dot_t(
                    q[g * stacked : (g + 1) * stacked], pair_ref[rows, g * HD : (g + 1) * HD]
                )
        column = lax.broadcasted_iota(jnp.int32, (heads * STEPS, window), 1)
        inverses = []
        logs = []
        for i in range(images):
            start = place_ref[2 * images + i]
            live = (column >= start) & (column < start + place_ref[3 * images + i])
            scores = jnp.where(live, score_s[i] * scale, FLOOR)
            peak = jnp.max(scores, axis=1, keepdims=True)
            weights = jnp.exp(scores - peak)
            total = jnp.sum(weights, axis=1, keepdims=True)
            weight_s[i] = weights.astype(jnp.bfloat16)
            inverses.append(1.0 / total)
            logs.append(jnp.broadcast_to(peak + jnp.log(total), (heads * STEPS, LANES)))
        lane = lax.broadcasted_iota(jnp.int32, (STEPS, LANES), 1)
        for i in range(images):
            rows = pl.ds(pl.multiple_of(place_ref[1 * images + i], 16), window)
            for g in range(kv_local):
                at = (kv_local + g) * HD
                part = dot(
                    weight_s[i, g * stacked : (g + 1) * stacked, :], pair_ref[rows, at : at + HD]
                )
                part = part * inverses[i][g * stacked : (g + 1) * stacked]
                for j in range(group):
                    h = g * group + j
                    out_ref[i, :, h * HD : (h + 1) * HD] = part[
                        j * STEPS : (j + 1) * STEPS
                    ].astype(out_ref.dtype)
            packed = jnp.zeros((STEPS, LANES), jnp.float32)
            for h in range(heads):
                log = logs[i][h * STEPS : (h + 1) * STEPS]
                packed = jnp.where(lane % heads == h, log, packed)
            out_ref[i, :, full:] = three_terms(packed, lane, heads)
            store = pltpu.make_async_copy(out_ref.at[i], out_hbm.at[place_ref[0 * images + i]], sems.at[i])
            store.start()
            stores.append(store)
        for store in stores:
            store.wait()

    anywhere = pl.BlockSpec(memory_space=pl.ANY)
    return pl.pallas_call(
        kernel,
        in_specs=[
            anywhere,
            pl.BlockSpec(memory_space=pltpu.VMEM),
        ]
        + [anywhere] * (1 + PIECES),
        out_specs=anywhere,
        out_shape=jax.ShapeDtypeStruct((slots, STEPS, full + LANES), queries.dtype),
        scratch_shapes=[
            pltpu.SMEM(places.shape, jnp.int32),
            pltpu.VMEM((count, columns), jnp.float32),
            pltpu.VMEM((count, columns), jnp.bfloat16),
            pltpu.VMEM((count, split), jnp.bfloat16),
            pltpu.VMEM((images, heads * STEPS, HD), jnp.float32),
            pltpu.VMEM((images, heads * STEPS, window), jnp.float32),
            pltpu.VMEM((images, heads * STEPS, window), jnp.bfloat16),
            pltpu.VMEM((images, STEPS, full + LANES), queries.dtype),
            pltpu.SemaphoreType.DMA,
            pltpu.SemaphoreType.DMA((2, PIECES)),
            pltpu.SemaphoreType.DMA((images,)),
        ],
        compiler_params=pltpu.CompilerParams(vmem_limit_bytes=32 << 20),
        name="visual_attention",
    )(places, queries, ours, *received)


def merge(slot_of_row, returned, cached, rows):
    full = cached.shape[2] - LANES
    heads = full // HD
    runs = 3 if rows % 3 == 0 else 1
    run = rows // runs

    def kernel(slot_hbm, returned_ref, cached_hbm, out_hbm, slot_ref, cached_s, out_s, slot_sem, sems):
        read_slots = pltpu.make_async_copy(slot_hbm, slot_ref, slot_sem)
        read_slots.start()
        loads = []
        stores = []
        for k in range(runs):
            span = pl.ds(k * run, run)
            load = pltpu.make_async_copy(cached_hbm.at[span], cached_s.at[span], sems.at[0, k])
            load.start()
            loads.append(load)
        read_slots.wait()
        for k in range(runs):
            loads[k].wait()
            for r in range(k * run, (k + 1) * run):
                present = slot_ref[r] >= 0
                slot = jnp.maximum(slot_ref[r], 0)
                terms = returned_ref[slot, :, full:].astype(jnp.float32)
                log = (
                    terms[:, :heads] + terms[:, heads : 2 * heads] + terms[:, 2 * heads : 3 * heads]
                )
                share = 1.0 / (1.0 + jnp.exp(cached_s[r, :, full : full + heads] - log))
                for h in range(heads):
                    lanes = slice(h * HD, (h + 1) * HD)
                    own = cached_s[r, :, lanes]
                    other = returned_ref[slot, :, lanes].astype(jnp.float32)
                    mixed = own + share[:, h : h + 1] * (other - own)
                    out_s[r, :, lanes] = jnp.where(present, mixed, own).astype(out_s.dtype)
            span = pl.ds(k * run, run)
            store = pltpu.make_async_copy(out_s.at[span], out_hbm.at[span], sems.at[1, k])
            store.start()
            stores.append(store)
        for store in stores:
            store.wait()

    anywhere = pl.BlockSpec(memory_space=pl.ANY)
    return pl.pallas_call(
        kernel,
        in_specs=[
            anywhere,
            pl.BlockSpec(memory_space=pltpu.VMEM),
            anywhere,
        ],
        out_specs=anywhere,
        out_shape=jax.ShapeDtypeStruct((rows, STEPS, full), jnp.bfloat16),
        scratch_shapes=[
            pltpu.SMEM(slot_of_row.shape, jnp.int32),
            pltpu.VMEM((rows, STEPS, full + LANES), jnp.float32),
            pltpu.VMEM((rows, STEPS, full), jnp.bfloat16),
            pltpu.SemaphoreType.DMA,
            pltpu.SemaphoreType.DMA((2, runs)),
        ],
        compiler_params=pltpu.CompilerParams(vmem_limit_bytes=32 << 20),
        name="merge",
    )(slot_of_row, returned, cached)


def shards(
    visual_tokens,
    kv_weight,
    image_lengths,
    image_owner,
    cache_lengths,
    cache_keys,
    cache_values,
    step_queries,
    step_keys,
    step_values,
):
    devices = lax.axis_size("dp")
    rows_local = cache_lengths.shape[0]
    images_local = image_lengths.shape[1]
    capacity = -(-rows_local // devices)
    weight_half = kv_weight[0]
    packed, slot_of_row = pack_queries(image_owner, step_queries, devices, capacity)
    tokens, packed = lax.optimization_barrier((visual_tokens, packed))
    asked = lax.all_to_all(packed, "dp", split_axis=0, concat_axis=0, tiled=True)
    for_partner, ours = project(tokens, weight_half)
    from_partner = [lax.ppermute(piece, "tensor", [(0, 1), (1, 0)]) for piece in for_partner]

    cached = cached_attention(
        step_queries, cache_keys, cache_values, step_keys, step_values, cache_lengths
    )

    device = lax.axis_index("dp")
    own_lengths = lax.dynamic_index_in_dim(image_lengths, device, 0, keepdims=False)
    own_device = (
        lax.dynamic_slice_in_dim(image_owner, device * images_local, images_local) // rows_local
    )
    order = jnp.arange(images_local)
    earlier = order[None, :] < order[:, None]
    own_rank = jnp.sum(
        ((own_device[:, None] == own_device[None, :]) & earlier).astype(jnp.int32), axis=1
    )
    starts = jnp.sum(jnp.where(earlier, own_lengths[None, :], 0), axis=1)
    window_at = jnp.minimum(starts // 16 * 16, visual_tokens.shape[0] - VMAX - 16)
    places = jnp.concatenate(
        [own_device * capacity + own_rank, window_at, starts - window_at, own_lengths]
    )

    answers = visual_attention(places, asked, ours, from_partner)
    returned = lax.all_to_all(answers, "dp", split_axis=0, concat_axis=0, tiled=True)
    return merge(slot_of_row, returned, cached, rows_local)


def solution(mesh):
    return jax.shard_map(
        shards,
        mesh=mesh,
        in_specs=(
            P(("groups", "dp"), "tensor"),
            P("tensor", None, None, None),
            P("groups", None),
            P("groups"),
            P(("groups", "dp")),
            P(("groups", "dp"), None, "tensor"),
            P(("groups", "dp"), None, "tensor"),
            P(("groups", "dp"), None, "tensor"),
            P(("groups", "dp"), None, "tensor"),
            P(("groups", "dp"), None, "tensor"),
        ),
        out_specs=P(("groups", "dp"), None, "tensor"),
        check_vma=False,
    )
```

```python
import jax
import jax.numpy as jnp
from jax import lax
from jax.experimental import pallas as pl
from jax.experimental.pallas import tpu as pltpu
from jax.sharding import PartitionSpec as P

D = 8192
HD = 128
STEPS = 4
VMAX = 48
EPSILON = 1e-06
LANES = 128
FLOOR = -1e30
RUNS = 4
ORDERS = {8: (5, 6, 4, 3, 1, 7, 2, 0)}
FAR_BYTES = 36 << 20


def exchange_order(devices):
    return ORDERS.get(devices, tuple(range(devices)))


def exchange(slots, devices):
    return lax.all_to_all(
        slots,
        "dp",
        split_axis=0,
        concat_axis=0,
        tiled=True,
        axis_index_groups=[list(exchange_order(devices))],
    )


def dot_t(a, b):
    return lax.dot_general(a, b, (((1,), (1,)), ((), ())), preferred_element_type=jnp.float32)


def dot(a, b):
    return jnp.dot(a, b, preferred_element_type=jnp.float32)


def three_terms(value, lane, step):
    first = value.astype(jnp.bfloat16).astype(jnp.float32)
    rest = value - first
    second = rest.astype(jnp.bfloat16).astype(jnp.float32)
    third = jnp.where(lane < 3 * step, rest - second, 0.0)
    terms = jnp.where(lane < step, first, jnp.where(lane < 2 * step, second, third))
    return terms.astype(jnp.bfloat16)


def pack_queries(image_owner, step_queries, devices, capacity):
    rows = step_queries.shape[0]
    images = image_owner.shape[0] // devices
    slots = devices * capacity
    table = (rows // LANES + 1) * LANES

    def kernel(
        owner_hbm, query_hbm, packed, slot_out, owner, queries, row_of_slot, slot_of_row, in_sems, sems
    ):
        read_owner = pltpu.make_async_copy(owner_hbm, owner, in_sems.at[0])
        read_queries = pltpu.make_async_copy(query_hbm, queries, in_sems.at[1])
        read_owner.start()
        read_queries.start()
        base = lax.axis_index("dp") * rows
        for r in range(rows):
            slot_of_row[r] = -1
        for slot in range(slots):
            row_of_slot[slot] = 0
        read_owner.wait()
        copies = []
        for place, s in enumerate(exchange_order(devices)):
            rank = jnp.int32(0)
            for i in range(images):
                row = owner[s * images + i] - base
                local = jnp.logical_and(row >= 0, row < rows)
                slot = place * capacity + rank
                row_of_slot[jnp.where(local, slot, slots)] = row
                slot_of_row[jnp.where(local, row, rows)] = slot
                rank = rank + local.astype(jnp.int32)
            if place == 0:
                read_queries.wait()
            for k in range(capacity):
                slot = place * capacity + k
                copy = pltpu.make_async_copy(
                    queries.at[row_of_slot[slot]], packed.at[slot], sems.at[slot]
                )
                copy.start()
                copies.append(copy)
        write_slots = pltpu.make_async_copy(slot_of_row, slot_out, in_sems.at[2])
        write_slots.start()
        for copy in copies:
            copy.wait()
        write_slots.wait()

    return pl.pallas_call(
        kernel,
        in_specs=[pl.BlockSpec(memory_space=pl.ANY), pl.BlockSpec(memory_space=pl.ANY)],
        out_specs=[pl.BlockSpec(memory_space=pl.ANY), pl.BlockSpec(memory_space=pl.ANY)],
        out_shape=[
            jax.ShapeDtypeStruct((slots,) + step_queries.shape[1:], step_queries.dtype),
            jax.ShapeDtypeStruct((table,), jnp.int32),
        ],
        scratch_shapes=[
            pltpu.SMEM(image_owner.shape, jnp.int32),
            pltpu.VMEM(step_queries.shape, step_queries.dtype),
            pltpu.SMEM((slots + 1,), jnp.int32),
            pltpu.SMEM((table,), jnp.int32),
            pltpu.SemaphoreType.DMA((3,)),
            pltpu.SemaphoreType.DMA((slots,)),
        ],
        name="pack_queries",
    )(image_owner, step_queries)


def project(tokens, weight):
    count, depth = tokens.shape
    width = weight.shape[2] // 2
    columns = 2 * width + LANES
    sizes = [512, 512] + [1024] * ((depth - 1024) // 1024)
    starts = [sum(sizes[:c]) for c in range(len(sizes))]
    chunks = len(sizes)
    ahead = 3

    def kernel(
        token_hbm, weight_hbm, theirs_ref, ours_hbm, ours_s, token_s, weight_s, sems, out_sem
    ):
        mine = lax.axis_index("tensor")

        def lanes(half):
            return pl.ds(pl.multiple_of(half * width, width), width)

        def product(x, w):
            w = jnp.swapaxes(w, 0, 1)
            return dot(x, jnp.concatenate([w[0], w[1]], axis=1))

        loads = []
        for c in range(chunks):
            span = pl.ds(starts[c], sizes[c])
            loads.append(
                [
                    pltpu.make_async_copy(
                        token_hbm.at[:, span], token_s.at[:, span], sems.at[0, c]
                    ),
                    pltpu.make_async_copy(
                        weight_hbm.at[span, :, lanes(mine)], weight_s.at[0, span], sems.at[1, c]
                    ),
                ]
            )
        loads.append(
            [
                pltpu.make_async_copy(
                    weight_hbm.at[:, :, lanes(1 - mine)], weight_s.at[1], sems.at[2, 0]
                )
            ]
        )

        def start(c):
            if c < len(loads):
                for load in loads[c]:
                    load.start()

        for c in range(ahead):
            start(c)
        squares = jnp.zeros((count, LANES), jnp.float32)
        for c in range(chunks):
            for load in loads[c]:
                load.wait()
            start(c + ahead)
            span = slice(starts[c], starts[c] + sizes[c])
            x = token_s[:, span]
            part = product(x, weight_s[0, span])
            if c == 0:
                ours_s[:, : 2 * width] = part
            else:
                ours_s[:, : 2 * width] += part
            for lane in range(0, sizes[c], LANES):
                wide = x[:, lane : lane + LANES].astype(jnp.float32)
                squares += wide * wide
        squares = jnp.broadcast_to(jnp.sum(squares, axis=1, keepdims=True), (count, LANES))
        ours_s[:, 2 * width :] = squares
        store = pltpu.make_async_copy(ours_s, ours_hbm.at[pl.ds(0, count)], out_sem)
        store.start()
        terms = three_terms(squares, lax.broadcasted_iota(jnp.int32, (count, LANES), 1), 1)
        for load in loads[chunks]:
            load.wait()
        theirs_ref[:, : 2 * width] = product(token_s[...], weight_s[1]).astype(jnp.bfloat16)
        theirs_ref[:, 2 * width :] = terms
        store.wait()

    hbm = pl.BlockSpec(memory_space=pltpu.HBM)
    return pl.pallas_call(
        kernel,
        in_specs=[hbm, hbm],
        out_specs=[pl.BlockSpec(memory_space=pltpu.VMEM), pl.BlockSpec(memory_space=pl.ANY)],
        out_shape=[
            jax.ShapeDtypeStruct((count, columns), jnp.bfloat16),
            jax.ShapeDtypeStruct((FAR_BYTES // (4 * columns), columns), jnp.float32),
        ],
        scratch_shapes=[
            pltpu.VMEM((count, columns), jnp.float32),
            pltpu.VMEM(tokens.shape, tokens.dtype),
            pltpu.VMEM((2, depth, 2, width), weight.dtype),
            pltpu.SemaphoreType.DMA((3, chunks)),
            pltpu.SemaphoreType.DMA,
        ],
        compiler_params=pltpu.CompilerParams(vmem_limit_bytes=60 << 20),
        cost_estimate=pl.CostEstimate(flops=1 << 20, bytes_accessed=1 << 16, transcendentals=0),
        name="project",
    )(tokens, weight)


def cached_attention(queries, cache_keys, cache_values, step_keys, step_values, lengths):
    rows, context, width = cache_keys.shape
    kv_local = width // HD
    heads = queries.shape[2] // HD
    group = heads // kv_local
    stacked = group * STEPS
    block = 8 if rows % 8 == 0 else 2
    scale = HD**-0.5

    def kernel(length_ref, q_ref, k_ref, v_ref, sk_ref, sv_ref, out_ref, q_s, sk_s, sv_s):
        first = pl.program_id(0) * block
        for r in range(block):
            for g in range(kv_local):
                sk_s[g, r * STEPS : (r + 1) * STEPS, :] = sk_ref[
                    r, :, g * HD : (g + 1) * HD
                ].astype(jnp.float32)
                sv_s[g, r * STEPS : (r + 1) * STEPS, :] = sv_ref[
                    r, :, g * HD : (g + 1) * HD
                ].astype(jnp.float32)
                for j in range(group):
                    h = g * group + j
                    at = r * stacked + j * STEPS
                    q_s[g, at : at + STEPS, :] = q_ref[r, :, h * HD : (h + 1) * HD].astype(
                        jnp.float32
                    )
        lane = lax.broadcasted_iota(jnp.int32, (STEPS, LANES), 1)
        logs = [jnp.zeros((STEPS, LANES), jnp.float32) for _ in range(block)]
        for g in range(kv_local):
            q = q_s[g].astype(jnp.bfloat16)
            steps = dot_t(q, sk_s[g].astype(jnp.bfloat16)) * scale
            at_row = lax.broadcasted_iota(jnp.int32, steps.shape, 0)
            at_key = lax.broadcasted_iota(jnp.int32, steps.shape, 1)
            own = (at_row // stacked == at_key // STEPS) & (at_key % STEPS <= at_row % STEPS)
            steps = jnp.where(own, steps, FLOOR)
            step_peak = jnp.max(steps, axis=1, keepdims=True)
            scores = []
            position = lax.broadcasted_iota(jnp.int32, (stacked, context), 1)
            for r in range(block):
                part = dot_t(q[r * stacked : (r + 1) * stacked], k_ref[r, :, g * HD : (g + 1) * HD])
                scores.append(jnp.where(position < length_ref[first + r], part * scale, FLOOR))
            cached = jnp.concatenate(scores, axis=0)
            peak = jnp.maximum(jnp.max(cached, axis=1, keepdims=True), step_peak)
            cached = jnp.exp(cached - peak)
            steps = jnp.where(own, jnp.exp(steps - peak), 0.0)
            total = jnp.sum(cached, axis=1, keepdims=True) + jnp.sum(steps, axis=1, keepdims=True)
            cached = cached.astype(jnp.bfloat16)
            mixed = dot(steps.astype(jnp.bfloat16), sv_s[g].astype(jnp.bfloat16))
            inverse = 1.0 / total
            log = jnp.broadcast_to(peak + jnp.log(total), (block * stacked, LANES))
            for r in range(block):
                span = slice(r * stacked, (r + 1) * stacked)
                part = dot(cached[span], v_ref[r, :, g * HD : (g + 1) * HD])
                part = (part + mixed[span]) * inverse[span]
                for j in range(group):
                    h = g * group + j
                    head = slice(j * STEPS, (j + 1) * STEPS)
                    out_ref[r * STEPS : (r + 1) * STEPS, h * HD : (h + 1) * HD] = part[head]
                    at = r * stacked + j * STEPS
                    logs[r] = jnp.where(lane == h, log[at : at + STEPS], logs[r])
        for r in range(block):
            out_ref[r * STEPS : (r + 1) * STEPS, heads * HD :] = logs[r]

    def spec(array):
        return pl.BlockSpec((block,) + array.shape[1:], lambda i, length_ref: (i, 0, 0))

    return pl.pallas_call(
        kernel,
        grid_spec=pltpu.PrefetchScalarGridSpec(
            num_scalar_prefetch=1,
            grid=(rows // block,),
            in_specs=[
                spec(queries),
                spec(cache_keys),
                spec(cache_values),
                spec(step_keys),
                spec(step_values),
            ],
            out_specs=pl.BlockSpec(
                (block * STEPS, heads * HD + LANES), lambda i, length_ref: (i, 0)
            ),
            scratch_shapes=[
                pltpu.VMEM((kv_local, block * stacked, HD), jnp.float32),
                pltpu.VMEM((kv_local, block * STEPS, HD), jnp.float32),
                pltpu.VMEM((kv_local, block * STEPS, HD), jnp.float32),
            ],
        ),
        out_shape=jax.ShapeDtypeStruct(
            (FAR_BYTES // (4 * (heads * HD + LANES)), heads * HD + LANES), jnp.float32
        ),
        compiler_params=pltpu.CompilerParams(vmem_limit_bytes=60 << 20),
        cost_estimate=pl.CostEstimate(flops=1 << 20, bytes_accessed=1 << 16, transcendentals=0),
        name="cached_attention",
    )(lengths, queries, cache_keys, cache_values, step_keys, step_values)


def visual_attention(places, queries, ours, received):
    images = places.shape[0] // 4
    slots, _, full = queries.shape
    heads = full // HD
    columns = ours.shape[1]
    split = columns - LANES
    kv_local = split // (2 * HD)
    count = received.shape[0]
    run = count // RUNS
    group = heads // kv_local
    stacked = group * STEPS
    window = VMAX + 16
    scale = HD**-0.5

    def kernel(
        place_hbm,
        q_ref,
        received_ref,
        ours_hbm,
        out_hbm,
        place_ref,
        ours_s,
        pair_ref,
        q_s,
        score_s,
        weight_s,
        out_ref,
        place_sem,
        load_sems,
        sems,
    ):
        read_places = pltpu.make_async_copy(place_hbm, place_ref, place_sem)
        read_places.start()
        loads = []
        for k in range(RUNS):
            rows = pl.ds(k * run, run)
            load = pltpu.make_async_copy(ours_hbm.at[rows], ours_s.at[rows], load_sems.at[k])
            load.start()
            loads.append(load)
        stores = []
        read_places.wait()
        for i in range(images):
            slot = place_ref[0 * images + i]
            for h in range(heads):
                q_s[i, h * STEPS : (h + 1) * STEPS, :] = q_ref[
                    slot, :, h * HD : (h + 1) * HD
                ].astype(jnp.float32)
        for k in range(RUNS):
            loads[k].wait()
            rows = slice(k * run, (k + 1) * run)
            squares = jnp.sum(
                received_ref[rows, split:].astype(jnp.float32), axis=1, keepdims=True
            )
            factor = lax.rsqrt((ours_s[rows, split:] + squares) / D + EPSILON)
            for at in range(0, split, LANES):
                lanes = slice(at, at + LANES)
                total = (ours_s[rows, lanes] + received_ref[rows, lanes].astype(jnp.float32)) * factor
                pair_ref[rows, lanes] = total.astype(pair_ref.dtype)
        for i in range(images):
            rows = pl.ds(pl.multiple_of(place_ref[1 * images + i], 16), window)
            q = q_s[i].astype(jnp.bfloat16)
            for g in range(kv_local):
                score_s[i, g * stacked : (g + 1) * stacked, :] = dot_t(
                    q[g * stacked : (g + 1) * stacked], pair_ref[rows, g * HD : (g + 1) * HD]
                )
        column = lax.broadcasted_iota(jnp.int32, (heads * STEPS, window), 1)
        inverses = []
        logs = []
        for i in range(images):
            start = place_ref[2 * images + i]
            live = (column >= start) & (column < start + place_ref[3 * images + i])
            scores = jnp.where(live, score_s[i] * scale, FLOOR)
            peak = jnp.max(scores, axis=1, keepdims=True)
            weights = jnp.exp(scores - peak)
            total = jnp.sum(weights, axis=1, keepdims=True)
            weight_s[i] = weights.astype(jnp.bfloat16)
            inverses.append(1.0 / total)
            logs.append(jnp.broadcast_to(peak + jnp.log(total), (heads * STEPS, LANES)))
        lane = lax.broadcasted_iota(jnp.int32, (STEPS, LANES), 1)
        for i in range(images):
            rows = pl.ds(pl.multiple_of(place_ref[1 * images + i], 16), window)
            for g in range(kv_local):
                at = (kv_local + g) * HD
                part = dot(
                    weight_s[i, g * stacked : (g + 1) * stacked, :], pair_ref[rows, at : at + HD]
                )
                part = part * inverses[i][g * stacked : (g + 1) * stacked]
                for j in range(group):
                    h = g * group + j
                    out_ref[i, :, h * HD : (h + 1) * HD] = part[
                        j * STEPS : (j + 1) * STEPS
                    ].astype(out_ref.dtype)
            packed = jnp.zeros((STEPS, LANES), jnp.float32)
            for h in range(heads):
                log = logs[i][h * STEPS : (h + 1) * STEPS]
                packed = jnp.where(lane % heads == h, log, packed)
            out_ref[i, :, full:] = three_terms(packed, lane, heads)
            store = pltpu.make_async_copy(out_ref.at[i], out_hbm.at[place_ref[0 * images + i]], sems.at[i])
            store.start()
            stores.append(store)
        for store in stores:
            store.wait()

    anywhere = pl.BlockSpec(memory_space=pl.ANY)
    vmem = pl.BlockSpec(memory_space=pltpu.VMEM)
    return pl.pallas_call(
        kernel,
        in_specs=[
            anywhere,
            vmem,
            vmem,
            anywhere,
        ],
        out_specs=anywhere,
        out_shape=jax.ShapeDtypeStruct((slots, STEPS, full + LANES), queries.dtype),
        scratch_shapes=[
            pltpu.SMEM(places.shape, jnp.int32),
            pltpu.VMEM((count, columns), jnp.float32),
            pltpu.VMEM((count, split), jnp.bfloat16),
            pltpu.VMEM((images, heads * STEPS, HD), jnp.float32),
            pltpu.VMEM((images, heads * STEPS, window), jnp.float32),
            pltpu.VMEM((images, heads * STEPS, window), jnp.bfloat16),
            pltpu.VMEM((images, STEPS, full + LANES), queries.dtype),
            pltpu.SemaphoreType.DMA,
            pltpu.SemaphoreType.DMA((RUNS,)),
            pltpu.SemaphoreType.DMA((images,)),
        ],
        compiler_params=pltpu.CompilerParams(vmem_limit_bytes=32 << 20),
        name="visual_attention",
    )(places, queries, received, ours)


def merge(slot_of_row, returned, cached, rows):
    full = cached.shape[1] - LANES
    heads = full // HD
    count = rows * STEPS
    block = 2 * STEPS
    runs = 3 if rows % 6 == 0 else 1
    run = count // runs

    def kernel(
        slot_hbm, returned_ref, cached_hbm, out_hbm, slot_ref, cached_s, other_s, out_s, slot_sem, sems
    ):
        read_slots = pltpu.make_async_copy(slot_hbm, slot_ref, slot_sem)
        read_slots.start()
        loads = []
        for k in range(runs):
            span = pl.ds(k * run, run)
            load = pltpu.make_async_copy(cached_hbm.at[span], cached_s.at[span], sems.at[0, k])
            load.start()
            loads.append(load)
        read_slots.wait()
        for r in range(rows):
            present = slot_ref[r] >= 0
            other = returned_ref[jnp.maximum(slot_ref[r], 0)].astype(jnp.float32)
            span = slice(r * STEPS, (r + 1) * STEPS)
            other_s[span, :full] = jnp.where(present, other[:, :full], 0.0)
            other_s[span, full:] = jnp.where(present, other[:, full:], FLOOR)
        stores = []
        for k in range(runs):
            loads[k].wait()
            for at in range(k * run, (k + 1) * run, block):
                span = slice(at, at + block)
                terms = other_s[span, full:]
                log = (
                    terms[:, :heads] + terms[:, heads : 2 * heads] + terms[:, 2 * heads : 3 * heads]
                )
                share = 1.0 / (1.0 + jnp.exp(cached_s[span, full : full + heads] - log))
                for h in range(heads):
                    lanes = slice(h * HD, (h + 1) * HD)
                    own = cached_s[span, lanes]
                    mixed = own + share[:, h : h + 1] * (other_s[span, lanes] - own)
                    mixed = mixed.astype(out_s.dtype).reshape(block // STEPS, STEPS, HD)
                    out_s[at // STEPS : (at + block) // STEPS, :, lanes] = mixed
            span = pl.ds(k * run // STEPS, run // STEPS)
            store = pltpu.make_async_copy(out_s.at[span], out_hbm.at[span], sems.at[1, k])
            store.start()
            stores.append(store)
        for store in stores:
            store.wait()

    anywhere = pl.BlockSpec(memory_space=pl.ANY)
    return pl.pallas_call(
        kernel,
        in_specs=[anywhere, pl.BlockSpec(memory_space=pltpu.VMEM), anywhere],
        out_specs=anywhere,
        out_shape=jax.ShapeDtypeStruct((rows, STEPS, full), jnp.bfloat16),
        scratch_shapes=[
            pltpu.SMEM(slot_of_row.shape, jnp.int32),
            pltpu.VMEM((count, full + LANES), jnp.float32),
            pltpu.VMEM((count, full + LANES), jnp.float32),
            pltpu.VMEM((rows, STEPS, full), jnp.bfloat16),
            pltpu.SemaphoreType.DMA,
            pltpu.SemaphoreType.DMA((2, runs)),
        ],
        compiler_params=pltpu.CompilerParams(vmem_limit_bytes=32 << 20),
        name="merge",
    )(slot_of_row, returned, cached)


def shards(
    visual_tokens,
    kv_weight,
    image_lengths,
    image_owner,
    cache_lengths,
    cache_keys,
    cache_values,
    step_queries,
    step_keys,
    step_values,
):
    devices = lax.axis_size("dp")
    rows_local = cache_lengths.shape[0]
    images_local = image_lengths.shape[1]
    capacity = -(-rows_local // devices)
    weight_half = kv_weight[0]
    packed, slot_of_row = pack_queries(image_owner, step_queries, devices, capacity)
    tokens, packed = lax.optimization_barrier((visual_tokens, packed))
    asked = exchange(packed, devices)
    for_partner, ours = project(tokens, weight_half)
    from_partner = lax.ppermute(for_partner, "tensor", [(0, 1), (1, 0)])

    cached = cached_attention(
        step_queries, cache_keys, cache_values, step_keys, step_values, cache_lengths
    )

    device = lax.axis_index("dp")
    own_lengths = lax.dynamic_index_in_dim(image_lengths, device, 0, keepdims=False)
    own_device = (
        lax.dynamic_slice_in_dim(image_owner, device * images_local, images_local) // rows_local
    )
    order = jnp.arange(images_local)
    earlier = order[None, :] < order[:, None]
    own_rank = jnp.sum(
        ((own_device[:, None] == own_device[None, :]) & earlier).astype(jnp.int32), axis=1
    )
    starts = jnp.sum(jnp.where(earlier, own_lengths[None, :], 0), axis=1)
    window_at = jnp.minimum(starts // 16 * 16, visual_tokens.shape[0] - VMAX - 16)
    order_of_place = jnp.array(exchange_order(devices), jnp.int32)
    own_place = jnp.sum(
        jnp.where(own_device[:, None] == order_of_place[None, :], jnp.arange(devices)[None, :], 0),
        axis=1,
    )
    places = jnp.concatenate(
        [own_place * capacity + own_rank, window_at, starts - window_at, own_lengths]
    )

    answers = visual_attention(places, asked, ours, from_partner)
    returned = exchange(answers, devices)
    return merge(slot_of_row, returned, cached, rows_local)


def solution(mesh):
    return jax.shard_map(
        shards,
        mesh=mesh,
        in_specs=(
            P(("groups", "dp"), "tensor"),
            P("tensor", None, None, None),
            P("groups", None),
            P("groups"),
            P(("groups", "dp")),
            P(("groups", "dp"), None, "tensor"),
            P(("groups", "dp"), None, "tensor"),
            P(("groups", "dp"), None, "tensor"),
            P(("groups", "dp"), None, "tensor"),
            P(("groups", "dp"), None, "tensor"),
        ),
        out_specs=P(("groups", "dp"), None, "tensor"),
        check_vma=False,
    )
```

```python
import jax
import jax.numpy as jnp
from jax import lax
from jax.experimental import pallas as pl
from jax.experimental.pallas import tpu as pltpu
from jax.sharding import PartitionSpec as P

D = 8192
HD = 128
STEPS = 4
VMAX = 48
EPSILON = 1e-06
LANES = 128
FLOOR = -1e30
RUNS = 2
ORDERS = {8: (5, 7, 4, 1, 3, 6, 2, 0)}
FAR_BYTES = 36 << 20


def exchange_order(devices):
    return ORDERS.get(devices, tuple(range(devices)))


def exchange(slots, devices):
    return lax.all_to_all(
        slots,
        "dp",
        split_axis=0,
        concat_axis=0,
        tiled=True,
        axis_index_groups=[list(exchange_order(devices))],
    )


def dot_t(a, b):
    return lax.dot_general(a, b, (((1,), (1,)), ((), ())), preferred_element_type=jnp.float32)


def dot(a, b):
    return jnp.dot(a, b, preferred_element_type=jnp.float32)


def three_terms(value, lane, step):
    first = value.astype(jnp.bfloat16).astype(jnp.float32)
    rest = value - first
    second = rest.astype(jnp.bfloat16).astype(jnp.float32)
    third = jnp.where(lane < 3 * step, rest - second, 0.0)
    terms = jnp.where(lane < step, first, jnp.where(lane < 2 * step, second, third))
    return terms.astype(jnp.bfloat16)


def pack_queries(image_owner, step_queries, devices, capacity):
    rows = step_queries.shape[0]
    images = image_owner.shape[0] // devices
    slots = devices * capacity
    table = (rows // LANES + 1) * LANES

    def kernel(
        owner_hbm, query_hbm, packed, slot_out, owner, queries, row_of_slot, slot_of_row, in_sems, sems
    ):
        read_owner = pltpu.make_async_copy(owner_hbm, owner, in_sems.at[0])
        read_queries = pltpu.make_async_copy(query_hbm, queries, in_sems.at[1])
        read_owner.start()
        read_queries.start()
        base = lax.axis_index("dp") * rows
        for r in range(rows):
            slot_of_row[r] = -1
        for slot in range(slots):
            row_of_slot[slot] = 0
        read_owner.wait()
        copies = []
        for place, s in enumerate(exchange_order(devices)):
            rank = jnp.int32(0)
            for i in range(images):
                row = owner[s * images + i] - base
                local = jnp.logical_and(row >= 0, row < rows)
                slot = place * capacity + rank
                row_of_slot[jnp.where(local, slot, slots)] = row
                slot_of_row[jnp.where(local, row, rows)] = slot
                rank = rank + local.astype(jnp.int32)
            if place == 0:
                read_queries.wait()
            for k in range(capacity):
                slot = place * capacity + k
                copy = pltpu.make_async_copy(
                    queries.at[row_of_slot[slot]], packed.at[slot], sems.at[slot]
                )
                copy.start()
                copies.append(copy)
        write_slots = pltpu.make_async_copy(slot_of_row, slot_out, in_sems.at[2])
        write_slots.start()
        for copy in copies:
            copy.wait()
        write_slots.wait()

    return pl.pallas_call(
        kernel,
        in_specs=[pl.BlockSpec(memory_space=pl.ANY), pl.BlockSpec(memory_space=pl.ANY)],
        out_specs=[pl.BlockSpec(memory_space=pl.ANY), pl.BlockSpec(memory_space=pl.ANY)],
        out_shape=[
            jax.ShapeDtypeStruct((slots,) + step_queries.shape[1:], step_queries.dtype),
            jax.ShapeDtypeStruct((table,), jnp.int32),
        ],
        scratch_shapes=[
            pltpu.SMEM(image_owner.shape, jnp.int32),
            pltpu.VMEM(step_queries.shape, step_queries.dtype),
            pltpu.SMEM((slots + 1,), jnp.int32),
            pltpu.SMEM((table,), jnp.int32),
            pltpu.SemaphoreType.DMA((3,)),
            pltpu.SemaphoreType.DMA((slots,)),
        ],
        name="pack_queries",
    )(image_owner, step_queries)


def project(tokens, weight):
    count, depth = tokens.shape
    width = weight.shape[2] // 2
    columns = 2 * width + LANES
    sizes = [512, 512] + [1024] * ((depth - 1024) // 1024)
    starts = [sum(sizes[:c]) for c in range(len(sizes))]
    chunks = len(sizes)
    ahead = 3

    def kernel(
        token_hbm, weight_hbm, theirs_ref, ours_hbm, ours_s, token_s, weight_s, sems, out_sem
    ):
        mine = lax.axis_index("tensor")

        def lanes(half):
            return pl.ds(pl.multiple_of(half * width, width), width)

        def product(x, w):
            w = jnp.swapaxes(w, 0, 1)
            return dot(x, jnp.concatenate([w[0], w[1]], axis=1))

        loads = []
        for c in range(chunks):
            span = pl.ds(starts[c], sizes[c])
            loads.append(
                [
                    pltpu.make_async_copy(
                        token_hbm.at[:, span], token_s.at[:, span], sems.at[0, c]
                    ),
                    pltpu.make_async_copy(
                        weight_hbm.at[span, :, lanes(mine)], weight_s.at[0, span], sems.at[1, c]
                    ),
                ]
            )
        loads.append(
            [
                pltpu.make_async_copy(
                    weight_hbm.at[:, :, lanes(1 - mine)], weight_s.at[1], sems.at[2, 0]
                )
            ]
        )

        def start(c):
            if c < len(loads):
                for load in loads[c]:
                    load.start()

        for c in range(ahead):
            start(c)
        squares = jnp.zeros((count, LANES), jnp.float32)
        for c in range(chunks):
            for load in loads[c]:
                load.wait()
            start(c + ahead)
            span = slice(starts[c], starts[c] + sizes[c])
            x = token_s[:, span]
            part = product(x, weight_s[0, span])
            if c == 0:
                ours_s[:, : 2 * width] = part
            else:
                ours_s[:, : 2 * width] += part
            for lane in range(0, sizes[c], LANES):
                wide = x[:, lane : lane + LANES].astype(jnp.float32)
                squares += wide * wide
        squares = jnp.broadcast_to(jnp.sum(squares, axis=1, keepdims=True), (count, LANES))
        ours_s[:, 2 * width :] = squares
        store = pltpu.make_async_copy(ours_s, ours_hbm.at[pl.ds(0, count)], out_sem)
        store.start()
        terms = three_terms(squares, lax.broadcasted_iota(jnp.int32, (count, LANES), 1), 1)
        for load in loads[chunks]:
            load.wait()
        theirs_ref[:, : 2 * width] = product(token_s[...], weight_s[1]).astype(jnp.bfloat16)
        theirs_ref[:, 2 * width :] = terms
        store.wait()

    hbm = pl.BlockSpec(memory_space=pltpu.HBM)
    return pl.pallas_call(
        kernel,
        in_specs=[hbm, hbm],
        out_specs=[pl.BlockSpec(memory_space=pltpu.VMEM), pl.BlockSpec(memory_space=pl.ANY)],
        out_shape=[
            jax.ShapeDtypeStruct((count, columns), jnp.bfloat16),
            jax.ShapeDtypeStruct((FAR_BYTES // (4 * columns), columns), jnp.float32),
        ],
        scratch_shapes=[
            pltpu.VMEM((count, columns), jnp.float32),
            pltpu.VMEM(tokens.shape, tokens.dtype),
            pltpu.VMEM((2, depth, 2, width), weight.dtype),
            pltpu.SemaphoreType.DMA((3, chunks)),
            pltpu.SemaphoreType.DMA,
        ],
        compiler_params=pltpu.CompilerParams(vmem_limit_bytes=60 << 20),
        cost_estimate=pl.CostEstimate(flops=1 << 20, bytes_accessed=1 << 16, transcendentals=0),
        name="project",
    )(tokens, weight)


def cached_attention(queries, cache_keys, cache_values, step_keys, step_values, lengths):
    rows, context, width = cache_keys.shape
    kv_local = width // HD
    heads = queries.shape[2] // HD
    group = heads // kv_local
    stacked = group * STEPS
    block = 8 if rows % 8 == 0 else 2
    scale = HD**-0.5

    def kernel(length_ref, q_ref, k_ref, v_ref, sk_ref, sv_ref, out_ref, q_s, sk_s, sv_s):
        first = pl.program_id(0) * block
        for r in range(block):
            for g in range(kv_local):
                sk_s[g, r * STEPS : (r + 1) * STEPS, :] = sk_ref[
                    r, :, g * HD : (g + 1) * HD
                ].astype(jnp.float32)
                sv_s[g, r * STEPS : (r + 1) * STEPS, :] = sv_ref[
                    r, :, g * HD : (g + 1) * HD
                ].astype(jnp.float32)
                for j in range(group):
                    h = g * group + j
                    at = r * stacked + j * STEPS
                    q_s[g, at : at + STEPS, :] = q_ref[r, :, h * HD : (h + 1) * HD].astype(
                        jnp.float32
                    )
        lane = lax.broadcasted_iota(jnp.int32, (STEPS, LANES), 1)
        logs = [jnp.zeros((STEPS, LANES), jnp.float32) for _ in range(block)]
        for g in range(kv_local):
            q = q_s[g].astype(jnp.bfloat16)
            steps = dot_t(q, sk_s[g].astype(jnp.bfloat16)) * scale
            at_row = lax.broadcasted_iota(jnp.int32, steps.shape, 0)
            at_key = lax.broadcasted_iota(jnp.int32, steps.shape, 1)
            own = (at_row // stacked == at_key // STEPS) & (at_key % STEPS <= at_row % STEPS)
            steps = jnp.where(own, steps, FLOOR)
            step_peak = jnp.max(steps, axis=1, keepdims=True)
            scores = []
            position = lax.broadcasted_iota(jnp.int32, (stacked, context), 1)
            for r in range(block):
                part = dot_t(q[r * stacked : (r + 1) * stacked], k_ref[r, :, g * HD : (g + 1) * HD])
                scores.append(jnp.where(position < length_ref[first + r], part * scale, FLOOR))
            cached = jnp.concatenate(scores, axis=0)
            peak = jnp.maximum(jnp.max(cached, axis=1, keepdims=True), step_peak)
            cached = jnp.exp(cached - peak)
            steps = jnp.where(own, jnp.exp(steps - peak), 0.0)
            total = jnp.sum(cached, axis=1, keepdims=True) + jnp.sum(steps, axis=1, keepdims=True)
            cached = cached.astype(jnp.bfloat16)
            mixed = dot(steps.astype(jnp.bfloat16), sv_s[g].astype(jnp.bfloat16))
            inverse = 1.0 / total
            log = jnp.broadcast_to(peak + jnp.log(total), (block * stacked, LANES))
            for r in range(block):
                span = slice(r * stacked, (r + 1) * stacked)
                part = dot(cached[span], v_ref[r, :, g * HD : (g + 1) * HD])
                part = (part + mixed[span]) * inverse[span]
                for j in range(group):
                    h = g * group + j
                    head = slice(j * STEPS, (j + 1) * STEPS)
                    out_ref[r * STEPS : (r + 1) * STEPS, h * HD : (h + 1) * HD] = part[head]
                    at = r * stacked + j * STEPS
                    logs[r] = jnp.where(lane == h, log[at : at + STEPS], logs[r])
        for r in range(block):
            out_ref[r * STEPS : (r + 1) * STEPS, heads * HD :] = logs[r]

    def spec(array):
        return pl.BlockSpec((block,) + array.shape[1:], lambda i, length_ref: (i, 0, 0))

    return pl.pallas_call(
        kernel,
        grid_spec=pltpu.PrefetchScalarGridSpec(
            num_scalar_prefetch=1,
            grid=(rows // block,),
            in_specs=[
                spec(queries),
                spec(cache_keys),
                spec(cache_values),
                spec(step_keys),
                spec(step_values),
            ],
            out_specs=pl.BlockSpec(
                (block * STEPS, heads * HD + LANES), lambda i, length_ref: (i, 0)
            ),
            scratch_shapes=[
                pltpu.VMEM((kv_local, block * stacked, HD), jnp.float32),
                pltpu.VMEM((kv_local, block * STEPS, HD), jnp.float32),
                pltpu.VMEM((kv_local, block * STEPS, HD), jnp.float32),
            ],
        ),
        out_shape=jax.ShapeDtypeStruct(
            (FAR_BYTES // (4 * (heads * HD + LANES)), heads * HD + LANES), jnp.float32
        ),
        compiler_params=pltpu.CompilerParams(vmem_limit_bytes=60 << 20),
        cost_estimate=pl.CostEstimate(flops=1 << 20, bytes_accessed=1 << 16, transcendentals=0),
        name="cached_attention",
    )(lengths, queries, cache_keys, cache_values, step_keys, step_values)


def visual_attention(places, queries, ours, received):
    images = places.shape[0] // 4
    slots, _, full = queries.shape
    heads = full // HD
    columns = ours.shape[1]
    split = columns - LANES
    kv_local = split // (2 * HD)
    count = received.shape[0]
    run = count // RUNS
    group = heads // kv_local
    stacked = group * STEPS
    window = VMAX + 16
    scale = HD**-0.5

    def kernel(
        place_hbm,
        q_ref,
        received_ref,
        ours_hbm,
        out_hbm,
        place_ref,
        ours_s,
        pair_ref,
        q_s,
        score_s,
        weight_s,
        out_ref,
        place_sem,
        load_sems,
        sems,
    ):
        read_places = pltpu.make_async_copy(place_hbm, place_ref, place_sem)
        read_places.start()
        loads = []
        for k in range(RUNS):
            rows = pl.ds(k * run, run)
            load = pltpu.make_async_copy(ours_hbm.at[rows], ours_s.at[rows], load_sems.at[k])
            load.start()
            loads.append(load)
        stores = []
        read_places.wait()
        for i in range(images):
            slot = place_ref[0 * images + i]
            for h in range(heads):
                q_s[i, h * STEPS : (h + 1) * STEPS, :] = q_ref[
                    slot, :, h * HD : (h + 1) * HD
                ].astype(jnp.float32)
        for k in range(RUNS):
            loads[k].wait()
            rows = slice(k * run, (k + 1) * run)
            squares = jnp.sum(
                received_ref[rows, split:].astype(jnp.float32), axis=1, keepdims=True
            )
            factor = lax.rsqrt((ours_s[rows, split:] + squares) / D + EPSILON)
            for at in range(0, split, LANES):
                lanes = slice(at, at + LANES)
                total = (ours_s[rows, lanes] + received_ref[rows, lanes].astype(jnp.float32)) * factor
                pair_ref[rows, lanes] = total.astype(pair_ref.dtype)
        for i in range(images):
            rows = pl.ds(pl.multiple_of(place_ref[1 * images + i], 16), window)
            q = q_s[i].astype(jnp.bfloat16)
            for g in range(kv_local):
                score_s[i, g * stacked : (g + 1) * stacked, :] = dot_t(
                    q[g * stacked : (g + 1) * stacked], pair_ref[rows, g * HD : (g + 1) * HD]
                )
        column = lax.broadcasted_iota(jnp.int32, (heads * STEPS, window), 1)
        inverses = []
        logs = []
        for i in range(images):
            start = place_ref[2 * images + i]
            live = (column >= start) & (column < start + place_ref[3 * images + i])
            scores = jnp.where(live, score_s[i] * scale, FLOOR)
            peak = jnp.max(scores, axis=1, keepdims=True)
            weights = jnp.exp(scores - peak)
            total = jnp.sum(weights, axis=1, keepdims=True)
            weight_s[i] = weights.astype(jnp.bfloat16)
            inverses.append(1.0 / total)
            logs.append(jnp.broadcast_to(peak + jnp.log(total), (heads * STEPS, LANES)))
        lane = lax.broadcasted_iota(jnp.int32, (STEPS, LANES), 1)
        for i in range(images):
            rows = pl.ds(pl.multiple_of(place_ref[1 * images + i], 16), window)
            for g in range(kv_local):
                at = (kv_local + g) * HD
                part = dot(
                    weight_s[i, g * stacked : (g + 1) * stacked, :], pair_ref[rows, at : at + HD]
                )
                part = part * inverses[i][g * stacked : (g + 1) * stacked]
                for j in range(group):
                    h = g * group + j
                    out_ref[i, :, h * HD : (h + 1) * HD] = part[
                        j * STEPS : (j + 1) * STEPS
                    ].astype(out_ref.dtype)
            packed = jnp.zeros((STEPS, LANES), jnp.float32)
            for h in range(heads):
                log = logs[i][h * STEPS : (h + 1) * STEPS]
                packed = jnp.where(lane % heads == h, log, packed)
            out_ref[i, :, full:] = three_terms(packed, lane, heads)
            store = pltpu.make_async_copy(out_ref.at[i], out_hbm.at[place_ref[0 * images + i]], sems.at[i])
            store.start()
            stores.append(store)
        for store in stores:
            store.wait()

    anywhere = pl.BlockSpec(memory_space=pl.ANY)
    vmem = pl.BlockSpec(memory_space=pltpu.VMEM)
    return pl.pallas_call(
        kernel,
        in_specs=[
            anywhere,
            vmem,
            vmem,
            anywhere,
        ],
        out_specs=anywhere,
        out_shape=jax.ShapeDtypeStruct((slots, STEPS, full + LANES), queries.dtype),
        scratch_shapes=[
            pltpu.SMEM(places.shape, jnp.int32),
            pltpu.VMEM((count, columns), jnp.float32),
            pltpu.VMEM((count, split), jnp.bfloat16),
            pltpu.VMEM((images, heads * STEPS, HD), jnp.float32),
            pltpu.VMEM((images, heads * STEPS, window), jnp.float32),
            pltpu.VMEM((images, heads * STEPS, window), jnp.bfloat16),
            pltpu.VMEM((images, STEPS, full + LANES), queries.dtype),
            pltpu.SemaphoreType.DMA,
            pltpu.SemaphoreType.DMA((RUNS,)),
            pltpu.SemaphoreType.DMA((images,)),
        ],
        compiler_params=pltpu.CompilerParams(vmem_limit_bytes=32 << 20),
        name="visual_attention",
    )(places, queries, received, ours)


def merge(slot_of_row, returned, cached, rows):
    full = cached.shape[1] - LANES
    heads = full // HD
    count = rows * STEPS
    block = 2 * STEPS
    runs = 3 if rows % 6 == 0 else 1
    run = count // runs

    def kernel(
        slot_hbm, returned_ref, cached_hbm, out_hbm, slot_ref, cached_s, other_s, out_s, slot_sem, sems
    ):
        read_slots = pltpu.make_async_copy(slot_hbm, slot_ref, slot_sem)
        read_slots.start()
        loads = []
        for k in range(runs):
            span = pl.ds(k * run, run)
            load = pltpu.make_async_copy(cached_hbm.at[span], cached_s.at[span], sems.at[0, k])
            load.start()
            loads.append(load)
        read_slots.wait()
        for r in range(rows):
            present = slot_ref[r] >= 0
            other = returned_ref[jnp.maximum(slot_ref[r], 0)].astype(jnp.float32)
            span = slice(r * STEPS, (r + 1) * STEPS)
            other_s[span, :full] = jnp.where(present, other[:, :full], 0.0)
            other_s[span, full:] = jnp.where(present, other[:, full:], FLOOR)
        stores = []
        for k in range(runs):
            loads[k].wait()
            for at in range(k * run, (k + 1) * run, block):
                span = slice(at, at + block)
                terms = other_s[span, full:]
                log = (
                    terms[:, :heads] + terms[:, heads : 2 * heads] + terms[:, 2 * heads : 3 * heads]
                )
                share = 1.0 / (1.0 + jnp.exp(cached_s[span, full : full + heads] - log))
                for h in range(heads):
                    lanes = slice(h * HD, (h + 1) * HD)
                    own = cached_s[span, lanes]
                    mixed = own + share[:, h : h + 1] * (other_s[span, lanes] - own)
                    mixed = mixed.astype(out_s.dtype).reshape(block // STEPS, STEPS, HD)
                    out_s[at // STEPS : (at + block) // STEPS, :, lanes] = mixed
            span = pl.ds(k * run // STEPS, run // STEPS)
            store = pltpu.make_async_copy(out_s.at[span], out_hbm.at[span], sems.at[1, k])
            store.start()
            stores.append(store)
        for store in stores:
            store.wait()

    anywhere = pl.BlockSpec(memory_space=pl.ANY)
    return pl.pallas_call(
        kernel,
        in_specs=[anywhere, pl.BlockSpec(memory_space=pltpu.VMEM), anywhere],
        out_specs=anywhere,
        out_shape=jax.ShapeDtypeStruct((rows, STEPS, full), jnp.bfloat16),
        scratch_shapes=[
            pltpu.SMEM(slot_of_row.shape, jnp.int32),
            pltpu.VMEM((count, full + LANES), jnp.float32),
            pltpu.VMEM((count, full + LANES), jnp.float32),
            pltpu.VMEM((rows, STEPS, full), jnp.bfloat16),
            pltpu.SemaphoreType.DMA,
            pltpu.SemaphoreType.DMA((2, runs)),
        ],
        compiler_params=pltpu.CompilerParams(vmem_limit_bytes=32 << 20),
        name="merge",
    )(slot_of_row, returned, cached)


def shards(
    visual_tokens,
    kv_weight,
    image_lengths,
    image_owner,
    cache_lengths,
    cache_keys,
    cache_values,
    step_queries,
    step_keys,
    step_values,
):
    devices = lax.axis_size("dp")
    rows_local = cache_lengths.shape[0]
    images_local = image_lengths.shape[1]
    capacity = -(-rows_local // devices)
    weight_half = kv_weight[0]
    packed, slot_of_row = pack_queries(image_owner, step_queries, devices, capacity)
    tokens, packed = lax.optimization_barrier((visual_tokens, packed))
    asked = exchange(packed, devices)
    for_partner, ours = project(tokens, weight_half)
    from_partner = lax.ppermute(for_partner, "tensor", [(0, 1), (1, 0)])

    cached = cached_attention(
        step_queries, cache_keys, cache_values, step_keys, step_values, cache_lengths
    )

    device = lax.axis_index("dp")
    own_lengths = lax.dynamic_index_in_dim(image_lengths, device, 0, keepdims=False)
    own_device = (
        lax.dynamic_slice_in_dim(image_owner, device * images_local, images_local) // rows_local
    )
    order = jnp.arange(images_local)
    earlier = order[None, :] < order[:, None]
    own_rank = jnp.sum(
        ((own_device[:, None] == own_device[None, :]) & earlier).astype(jnp.int32), axis=1
    )
    starts = jnp.sum(jnp.where(earlier, own_lengths[None, :], 0), axis=1)
    window_at = jnp.minimum(starts // 16 * 16, visual_tokens.shape[0] - VMAX - 16)
    order_of_place = jnp.array(exchange_order(devices), jnp.int32)
    own_place = jnp.sum(
        jnp.where(own_device[:, None] == order_of_place[None, :], jnp.arange(devices)[None, :], 0),
        axis=1,
    )
    places = jnp.concatenate(
        [own_place * capacity + own_rank, window_at, starts - window_at, own_lengths]
    )

    answers = visual_attention(places, asked, ours, from_partner)
    returned = exchange(answers, devices)
    return merge(slot_of_row, returned, cached, rows_local)


def solution(mesh):
    return jax.shard_map(
        shards,
        mesh=mesh,
        in_specs=(
            P(("groups", "dp"), "tensor"),
            P("tensor", None, None, None),
            P("groups", None),
            P("groups"),
            P(("groups", "dp")),
            P(("groups", "dp"), None, "tensor"),
            P(("groups", "dp"), None, "tensor"),
            P(("groups", "dp"), None, "tensor"),
            P(("groups", "dp"), None, "tensor"),
            P(("groups", "dp"), None, "tensor"),
        ),
        out_specs=P(("groups", "dp"), None, "tensor"),
        check_vma=False,
    )
```

```python
import jax
import jax.numpy as jnp
from jax import lax
from jax.experimental import pallas as pl
from jax.experimental.pallas import tpu as pltpu
from jax.sharding import PartitionSpec as P

D = 8192
HD = 128
STEPS = 4
VMAX = 48
EPSILON = 1e-06
LANES = 128
FLOOR = -1e30
RUNS = 2
ORDERS = {8: (5, 7, 4, 1, 3, 6, 2, 0)}
FAR_BYTES = 36 << 20


def exchange_order(devices):
    return ORDERS.get(devices, tuple(range(devices)))


def exchange(slots, devices):
    return lax.all_to_all(
        slots,
        "dp",
        split_axis=0,
        concat_axis=0,
        tiled=True,
        axis_index_groups=[list(exchange_order(devices))],
    )


def dot_t(a, b):
    return lax.dot_general(a, b, (((1,), (1,)), ((), ())), preferred_element_type=jnp.float32)


def dot(a, b):
    return jnp.dot(a, b, preferred_element_type=jnp.float32)


def three_terms(value, lane, step):
    first = value.astype(jnp.bfloat16).astype(jnp.float32)
    rest = value - first
    second = rest.astype(jnp.bfloat16).astype(jnp.float32)
    third = jnp.where(lane < 3 * step, rest - second, 0.0)
    terms = jnp.where(lane < step, first, jnp.where(lane < 2 * step, second, third))
    return terms.astype(jnp.bfloat16)


def pack_queries(image_owner, step_queries, devices, capacity):
    rows = step_queries.shape[0]
    images = image_owner.shape[0] // devices
    slots = devices * capacity
    table = (rows // LANES + 1) * LANES

    def kernel(
        owner_hbm, query_hbm, packed, slot_out, owner, queries, row_of_slot, slot_of_row, in_sems, sems
    ):
        read_owner = pltpu.make_async_copy(owner_hbm, owner, in_sems.at[0])
        read_queries = pltpu.make_async_copy(query_hbm, queries, in_sems.at[1])
        read_owner.start()
        read_queries.start()
        base = lax.axis_index("dp") * rows
        for r in range(rows):
            slot_of_row[r] = -1
        for slot in range(slots):
            row_of_slot[slot] = 0
        read_owner.wait()
        copies = []
        for place, s in enumerate(exchange_order(devices)):
            rank = jnp.int32(0)
            for i in range(images):
                row = owner[s * images + i] - base
                local = jnp.logical_and(row >= 0, row < rows)
                slot = place * capacity + rank
                row_of_slot[jnp.where(local, slot, slots)] = row
                slot_of_row[jnp.where(local, row, rows)] = slot
                rank = rank + local.astype(jnp.int32)
            if place == 0:
                read_queries.wait()
            for k in range(capacity):
                slot = place * capacity + k
                copy = pltpu.make_async_copy(
                    queries.at[row_of_slot[slot]], packed.at[slot], sems.at[slot]
                )
                copy.start()
                copies.append(copy)
        write_slots = pltpu.make_async_copy(slot_of_row, slot_out, in_sems.at[2])
        write_slots.start()
        for copy in copies:
            copy.wait()
        write_slots.wait()

    return pl.pallas_call(
        kernel,
        in_specs=[pl.BlockSpec(memory_space=pl.ANY), pl.BlockSpec(memory_space=pl.ANY)],
        out_specs=[pl.BlockSpec(memory_space=pl.ANY), pl.BlockSpec(memory_space=pl.ANY)],
        out_shape=[
            jax.ShapeDtypeStruct((slots,) + step_queries.shape[1:], step_queries.dtype),
            jax.ShapeDtypeStruct((table,), jnp.int32),
        ],
        scratch_shapes=[
            pltpu.SMEM(image_owner.shape, jnp.int32),
            pltpu.VMEM(step_queries.shape, step_queries.dtype),
            pltpu.SMEM((slots + 1,), jnp.int32),
            pltpu.SMEM((table,), jnp.int32),
            pltpu.SemaphoreType.DMA((3,)),
            pltpu.SemaphoreType.DMA((slots,)),
        ],
        name="pack_queries",
    )(image_owner, step_queries)


def project(tokens, weight):
    count, depth = tokens.shape
    width = weight.shape[2] // 2
    columns = 2 * width + LANES
    sizes = [512, 512] + [1024] * ((depth - 1024) // 1024)
    starts = [sum(sizes[:c]) for c in range(len(sizes))]
    chunks = len(sizes)
    ahead = 3

    def kernel(
        token_hbm, weight_hbm, theirs_ref, ours_hbm, total_s, ours_s, token_s, weight_s, sems, out_sem
    ):
        mine = lax.axis_index("tensor")

        def lanes(half):
            return pl.ds(pl.multiple_of(half * width, width), width)

        def product(x, w):
            w = jnp.swapaxes(w, 0, 1)
            return dot(x, jnp.concatenate([w[0], w[1]], axis=1))

        loads = []
        for c in range(chunks):
            span = pl.ds(starts[c], sizes[c])
            loads.append(
                [
                    pltpu.make_async_copy(
                        token_hbm.at[:, span], token_s.at[:, span], sems.at[0, c]
                    ),
                    pltpu.make_async_copy(
                        weight_hbm.at[span, :, lanes(mine)], weight_s.at[0, span], sems.at[1, c]
                    ),
                ]
            )
        loads.append(
            [
                pltpu.make_async_copy(
                    weight_hbm.at[:, :, lanes(1 - mine)], weight_s.at[1], sems.at[2, 0]
                )
            ]
        )

        def start(c):
            if c < len(loads):
                for load in loads[c]:
                    load.start()

        for c in range(ahead):
            start(c)
        squares = jnp.zeros((count, LANES), jnp.float32)
        for c in range(chunks):
            for load in loads[c]:
                load.wait()
            start(c + ahead)
            span = slice(starts[c], starts[c] + sizes[c])
            x = token_s[:, span]
            part = product(x, weight_s[0, span])
            if c == 0:
                total_s[...] = part
            else:
                total_s[...] += part
            for lane in range(0, sizes[c], LANES):
                wide = x[:, lane : lane + LANES].astype(jnp.float32)
                squares += wide * wide
        squares = jnp.broadcast_to(jnp.sum(squares, axis=1, keepdims=True), (count, LANES))
        terms = three_terms(squares, lax.broadcasted_iota(jnp.int32, (count, LANES), 1), 1)
        ours_s[:, : 2 * width] = total_s[...].astype(jnp.bfloat16)
        ours_s[:, 2 * width :] = terms
        store = pltpu.make_async_copy(ours_s, ours_hbm.at[pl.ds(0, count)], out_sem)
        store.start()
        for load in loads[chunks]:
            load.wait()
        theirs_ref[:, : 2 * width] = product(token_s[...], weight_s[1]).astype(jnp.bfloat16)
        theirs_ref[:, 2 * width :] = terms
        store.wait()

    hbm = pl.BlockSpec(memory_space=pltpu.HBM)
    return pl.pallas_call(
        kernel,
        in_specs=[hbm, hbm],
        out_specs=[pl.BlockSpec(memory_space=pltpu.VMEM), pl.BlockSpec(memory_space=pl.ANY)],
        out_shape=[
            jax.ShapeDtypeStruct((count, columns), jnp.bfloat16),
            jax.ShapeDtypeStruct((FAR_BYTES // (2 * columns), columns), jnp.bfloat16),
        ],
        scratch_shapes=[
            pltpu.VMEM((count, 2 * width), jnp.float32),
            pltpu.VMEM((count, columns), jnp.bfloat16),
            pltpu.VMEM(tokens.shape, tokens.dtype),
            pltpu.VMEM((2, depth, 2, width), weight.dtype),
            pltpu.SemaphoreType.DMA((3, chunks)),
            pltpu.SemaphoreType.DMA,
        ],
        compiler_params=pltpu.CompilerParams(vmem_limit_bytes=60 << 20),
        cost_estimate=pl.CostEstimate(flops=1 << 20, bytes_accessed=1 << 16, transcendentals=0),
        name="project",
    )(tokens, weight)


def cached_attention(queries, cache_keys, cache_values, step_keys, step_values, lengths):
    rows, context, width = cache_keys.shape
    kv_local = width // HD
    heads = queries.shape[2] // HD
    group = heads // kv_local
    stacked = group * STEPS
    block = 8 if rows % 8 == 0 else 2
    scale = HD**-0.5

    def kernel(length_ref, q_ref, k_ref, v_ref, sk_ref, sv_ref, out_ref, q_s, sk_s, sv_s):
        first = pl.program_id(0) * block
        for r in range(block):
            for g in range(kv_local):
                sk_s[g, r * STEPS : (r + 1) * STEPS, :] = sk_ref[
                    r, :, g * HD : (g + 1) * HD
                ].astype(jnp.float32)
                sv_s[g, r * STEPS : (r + 1) * STEPS, :] = sv_ref[
                    r, :, g * HD : (g + 1) * HD
                ].astype(jnp.float32)
                for j in range(group):
                    h = g * group + j
                    at = r * stacked + j * STEPS
                    q_s[g, at : at + STEPS, :] = q_ref[r, :, h * HD : (h + 1) * HD].astype(
                        jnp.float32
                    )
        lane = lax.broadcasted_iota(jnp.int32, (STEPS, LANES), 1)
        logs = [jnp.zeros((STEPS, LANES), jnp.float32) for _ in range(block)]
        for g in range(kv_local):
            q = q_s[g].astype(jnp.bfloat16)
            steps = dot_t(q, sk_s[g].astype(jnp.bfloat16)) * scale
            at_row = lax.broadcasted_iota(jnp.int32, steps.shape, 0)
            at_key = lax.broadcasted_iota(jnp.int32, steps.shape, 1)
            own = (at_row // stacked == at_key // STEPS) & (at_key % STEPS <= at_row % STEPS)
            steps = jnp.where(own, steps, FLOOR)
            step_peak = jnp.max(steps, axis=1, keepdims=True)
            scores = []
            position = lax.broadcasted_iota(jnp.int32, (stacked, context), 1)
            for r in range(block):
                part = dot_t(q[r * stacked : (r + 1) * stacked], k_ref[r, :, g * HD : (g + 1) * HD])
                scores.append(jnp.where(position < length_ref[first + r], part * scale, FLOOR))
            cached = jnp.concatenate(scores, axis=0)
            peak = jnp.maximum(jnp.max(cached, axis=1, keepdims=True), step_peak)
            cached = jnp.exp(cached - peak)
            steps = jnp.where(own, jnp.exp(steps - peak), 0.0)
            total = jnp.sum(cached, axis=1, keepdims=True) + jnp.sum(steps, axis=1, keepdims=True)
            cached = cached.astype(jnp.bfloat16)
            mixed = dot(steps.astype(jnp.bfloat16), sv_s[g].astype(jnp.bfloat16))
            inverse = 1.0 / total
            log = jnp.broadcast_to(peak + jnp.log(total), (block * stacked, LANES))
            for r in range(block):
                span = slice(r * stacked, (r + 1) * stacked)
                part = dot(cached[span], v_ref[r, :, g * HD : (g + 1) * HD])
                part = (part + mixed[span]) * inverse[span]
                for j in range(group):
                    h = g * group + j
                    head = slice(j * STEPS, (j + 1) * STEPS)
                    out_ref[r * STEPS : (r + 1) * STEPS, h * HD : (h + 1) * HD] = part[head]
                    at = r * stacked + j * STEPS
                    logs[r] = jnp.where(lane == h, log[at : at + STEPS], logs[r])
        for r in range(block):
            out_ref[r * STEPS : (r + 1) * STEPS, heads * HD :] = logs[r]

    def spec(array):
        return pl.BlockSpec((block,) + array.shape[1:], lambda i, length_ref: (i, 0, 0))

    return pl.pallas_call(
        kernel,
        grid_spec=pltpu.PrefetchScalarGridSpec(
            num_scalar_prefetch=1,
            grid=(rows // block,),
            in_specs=[
                spec(queries),
                spec(cache_keys),
                spec(cache_values),
                spec(step_keys),
                spec(step_values),
            ],
            out_specs=pl.BlockSpec(
                (block * STEPS, heads * HD + LANES), lambda i, length_ref: (i, 0)
            ),
            scratch_shapes=[
                pltpu.VMEM((kv_local, block * stacked, HD), jnp.float32),
                pltpu.VMEM((kv_local, block * STEPS, HD), jnp.float32),
                pltpu.VMEM((kv_local, block * STEPS, HD), jnp.float32),
            ],
        ),
        out_shape=jax.ShapeDtypeStruct(
            (FAR_BYTES // (4 * (heads * HD + LANES)), heads * HD + LANES), jnp.float32
        ),
        compiler_params=pltpu.CompilerParams(vmem_limit_bytes=60 << 20),
        cost_estimate=pl.CostEstimate(flops=1 << 20, bytes_accessed=1 << 16, transcendentals=0),
        name="cached_attention",
    )(lengths, queries, cache_keys, cache_values, step_keys, step_values)


def visual_attention(places, queries, ours, received):
    images = places.shape[0] // 4
    slots, _, full = queries.shape
    heads = full // HD
    columns = ours.shape[1]
    split = columns - LANES
    kv_local = split // (2 * HD)
    count = received.shape[0]
    run = count // RUNS
    group = heads // kv_local
    stacked = group * STEPS
    window = VMAX + 16
    scale = HD**-0.5

    def kernel(
        place_hbm,
        q_ref,
        received_ref,
        ours_hbm,
        out_hbm,
        place_ref,
        ours_s,
        pair_ref,
        q_s,
        score_s,
        weight_s,
        out_ref,
        place_sem,
        load_sems,
        sems,
    ):
        read_places = pltpu.make_async_copy(place_hbm, place_ref, place_sem)
        read_places.start()
        loads = []
        for k in range(RUNS):
            rows = pl.ds(k * run, run)
            load = pltpu.make_async_copy(ours_hbm.at[rows], ours_s.at[rows], load_sems.at[k])
            load.start()
            loads.append(load)
        stores = []
        read_places.wait()
        for i in range(images):
            slot = place_ref[0 * images + i]
            for h in range(heads):
                q_s[i, h * STEPS : (h + 1) * STEPS, :] = q_ref[
                    slot, :, h * HD : (h + 1) * HD
                ].astype(jnp.float32)
        for k in range(RUNS):
            loads[k].wait()
            rows = slice(k * run, (k + 1) * run)
            squares = ours_s[rows, split:].astype(jnp.float32) + received_ref[
                rows, split:
            ].astype(jnp.float32)
            factor = lax.rsqrt(jnp.sum(squares, axis=1, keepdims=True) / D + EPSILON)
            for at in range(0, split, LANES):
                lanes = slice(at, at + LANES)
                total = ours_s[rows, lanes].astype(jnp.float32) + received_ref[rows, lanes].astype(
                    jnp.float32
                )
                pair_ref[rows, lanes] = (total * factor).astype(pair_ref.dtype)
        for i in range(images):
            rows = pl.ds(pl.multiple_of(place_ref[1 * images + i], 16), window)
            q = q_s[i].astype(jnp.bfloat16)
            for g in range(kv_local):
                score_s[i, g * stacked : (g + 1) * stacked, :] = dot_t(
                    q[g * stacked : (g + 1) * stacked], pair_ref[rows, g * HD : (g + 1) * HD]
                )
        column = lax.broadcasted_iota(jnp.int32, (heads * STEPS, window), 1)
        inverses = []
        logs = []
        for i in range(images):
            start = place_ref[2 * images + i]
            live = (column >= start) & (column < start + place_ref[3 * images + i])
            scores = jnp.where(live, score_s[i] * scale, FLOOR)
            peak = jnp.max(scores, axis=1, keepdims=True)
            weights = jnp.exp(scores - peak)
            total = jnp.sum(weights, axis=1, keepdims=True)
            weight_s[i] = weights.astype(jnp.bfloat16)
            inverses.append(1.0 / total)
            logs.append(jnp.broadcast_to(peak + jnp.log(total), (heads * STEPS, LANES)))
        lane = lax.broadcasted_iota(jnp.int32, (STEPS, LANES), 1)
        for i in range(images):
            rows = pl.ds(pl.multiple_of(place_ref[1 * images + i], 16), window)
            for g in range(kv_local):
                at = (kv_local + g) * HD
                part = dot(
                    weight_s[i, g * stacked : (g + 1) * stacked, :], pair_ref[rows, at : at + HD]
                )
                part = part * inverses[i][g * stacked : (g + 1) * stacked]
                for j in range(group):
                    h = g * group + j
                    out_ref[i, :, h * HD : (h + 1) * HD] = part[
                        j * STEPS : (j + 1) * STEPS
                    ].astype(out_ref.dtype)
            packed = jnp.zeros((STEPS, LANES), jnp.float32)
            for h in range(heads):
                log = logs[i][h * STEPS : (h + 1) * STEPS]
                packed = jnp.where(lane % heads == h, log, packed)
            out_ref[i, :, full:] = three_terms(packed, lane, heads)
            store = pltpu.make_async_copy(out_ref.at[i], out_hbm.at[place_ref[0 * images + i]], sems.at[i])
            store.start()
            stores.append(store)
        for store in stores:
            store.wait()

    anywhere = pl.BlockSpec(memory_space=pl.ANY)
    vmem = pl.BlockSpec(memory_space=pltpu.VMEM)
    return pl.pallas_call(
        kernel,
        in_specs=[
            anywhere,
            vmem,
            vmem,
            anywhere,
        ],
        out_specs=anywhere,
        out_shape=jax.ShapeDtypeStruct((slots, STEPS, full + LANES), queries.dtype),
        scratch_shapes=[
            pltpu.SMEM(places.shape, jnp.int32),
            pltpu.VMEM((count, columns), jnp.bfloat16),
            pltpu.VMEM((count, split), jnp.bfloat16),
            pltpu.VMEM((images, heads * STEPS, HD), jnp.float32),
            pltpu.VMEM((images, heads * STEPS, window), jnp.float32),
            pltpu.VMEM((images, heads * STEPS, window), jnp.bfloat16),
            pltpu.VMEM((images, STEPS, full + LANES), queries.dtype),
            pltpu.SemaphoreType.DMA,
            pltpu.SemaphoreType.DMA((RUNS,)),
            pltpu.SemaphoreType.DMA((images,)),
        ],
        compiler_params=pltpu.CompilerParams(vmem_limit_bytes=32 << 20),
        name="visual_attention",
    )(places, queries, received, ours)


def merge(slot_of_row, returned, cached, rows):
    full = cached.shape[1] - LANES
    heads = full // HD
    count = rows * STEPS
    block = 2 * STEPS
    runs = 3 if rows % 6 == 0 else 1
    run = count // runs

    def kernel(
        slot_hbm, returned_ref, cached_hbm, out_hbm, slot_ref, cached_s, other_s, out_s, slot_sem, sems
    ):
        read_slots = pltpu.make_async_copy(slot_hbm, slot_ref, slot_sem)
        read_slots.start()
        loads = []
        for k in range(runs):
            span = pl.ds(k * run, run)
            load = pltpu.make_async_copy(cached_hbm.at[span], cached_s.at[span], sems.at[0, k])
            load.start()
            loads.append(load)
        read_slots.wait()
        for r in range(rows):
            present = slot_ref[r] >= 0
            other = returned_ref[jnp.maximum(slot_ref[r], 0)].astype(jnp.float32)
            span = slice(r * STEPS, (r + 1) * STEPS)
            other_s[span, :full] = jnp.where(present, other[:, :full], 0.0)
            other_s[span, full:] = jnp.where(present, other[:, full:], FLOOR)
        stores = []
        for k in range(runs):
            loads[k].wait()
            for at in range(k * run, (k + 1) * run, block):
                span = slice(at, at + block)
                terms = other_s[span, full:]
                log = (
                    terms[:, :heads] + terms[:, heads : 2 * heads] + terms[:, 2 * heads : 3 * heads]
                )
                share = 1.0 / (1.0 + jnp.exp(cached_s[span, full : full + heads] - log))
                for h in range(heads):
                    lanes = slice(h * HD, (h + 1) * HD)
                    own = cached_s[span, lanes]
                    mixed = own + share[:, h : h + 1] * (other_s[span, lanes] - own)
                    mixed = mixed.astype(out_s.dtype).reshape(block // STEPS, STEPS, HD)
                    out_s[at // STEPS : (at + block) // STEPS, :, lanes] = mixed
            span = pl.ds(k * run // STEPS, run // STEPS)
            store = pltpu.make_async_copy(out_s.at[span], out_hbm.at[span], sems.at[1, k])
            store.start()
            stores.append(store)
        for store in stores:
            store.wait()

    anywhere = pl.BlockSpec(memory_space=pl.ANY)
    return pl.pallas_call(
        kernel,
        in_specs=[anywhere, pl.BlockSpec(memory_space=pltpu.VMEM), anywhere],
        out_specs=anywhere,
        out_shape=jax.ShapeDtypeStruct((rows, STEPS, full), jnp.bfloat16),
        scratch_shapes=[
            pltpu.SMEM(slot_of_row.shape, jnp.int32),
            pltpu.VMEM((count, full + LANES), jnp.float32),
            pltpu.VMEM((count, full + LANES), jnp.float32),
            pltpu.VMEM((rows, STEPS, full), jnp.bfloat16),
            pltpu.SemaphoreType.DMA,
            pltpu.SemaphoreType.DMA((2, runs)),
        ],
        compiler_params=pltpu.CompilerParams(vmem_limit_bytes=32 << 20),
        name="merge",
    )(slot_of_row, returned, cached)


def shards(
    visual_tokens,
    kv_weight,
    image_lengths,
    image_owner,
    cache_lengths,
    cache_keys,
    cache_values,
    step_queries,
    step_keys,
    step_values,
):
    devices = lax.axis_size("dp")
    rows_local = cache_lengths.shape[0]
    images_local = image_lengths.shape[1]
    capacity = -(-rows_local // devices)
    weight_half = kv_weight[0]
    packed, slot_of_row = pack_queries(image_owner, step_queries, devices, capacity)
    tokens, packed = lax.optimization_barrier((visual_tokens, packed))
    asked = exchange(packed, devices)
    for_partner, ours = project(tokens, weight_half)
    from_partner = lax.ppermute(for_partner, "tensor", [(0, 1), (1, 0)])

    cached = cached_attention(
        step_queries, cache_keys, cache_values, step_keys, step_values, cache_lengths
    )

    device = lax.axis_index("dp")
    own_lengths = lax.dynamic_index_in_dim(image_lengths, device, 0, keepdims=False)
    own_device = (
        lax.dynamic_slice_in_dim(image_owner, device * images_local, images_local) // rows_local
    )
    order = jnp.arange(images_local)
    earlier = order[None, :] < order[:, None]
    own_rank = jnp.sum(
        ((own_device[:, None] == own_device[None, :]) & earlier).astype(jnp.int32), axis=1
    )
    starts = jnp.sum(jnp.where(earlier, own_lengths[None, :], 0), axis=1)
    window_at = jnp.minimum(starts // 16 * 16, visual_tokens.shape[0] - VMAX - 16)
    order_of_place = jnp.array(exchange_order(devices), jnp.int32)
    own_place = jnp.sum(
        jnp.where(own_device[:, None] == order_of_place[None, :], jnp.arange(devices)[None, :], 0),
        axis=1,
    )
    places = jnp.concatenate(
        [own_place * capacity + own_rank, window_at, starts - window_at, own_lengths]
    )

    answers = visual_attention(places, asked, ours, from_partner)
    returned = exchange(answers, devices)
    return merge(slot_of_row, returned, cached, rows_local)


def solution(mesh):
    return jax.shard_map(
        shards,
        mesh=mesh,
        in_specs=(
            P(("groups", "dp"), "tensor"),
            P("tensor", None, None, None),
            P("groups", None),
            P("groups"),
            P(("groups", "dp")),
            P(("groups", "dp"), None, "tensor"),
            P(("groups", "dp"), None, "tensor"),
            P(("groups", "dp"), None, "tensor"),
            P(("groups", "dp"), None, "tensor"),
            P(("groups", "dp"), None, "tensor"),
        ),
        out_specs=P(("groups", "dp"), None, "tensor"),
        check_vma=False,
    )
```

```python
import jax
import jax.numpy as jnp
from jax import lax
from jax.experimental import pallas as pl
from jax.experimental.pallas import tpu as pltpu
from jax.sharding import PartitionSpec as P

D = 8192
HD = 128
STEPS = 4
VMAX = 48
EPSILON = 1e-06
LANES = 128
FLOOR = -1e30
RUNS = 1
ORDERS = {8: (5, 7, 4, 1, 3, 6, 2, 0)}
FAR_BYTES = 36 << 20


def exchange_order(devices):
    return ORDERS.get(devices, tuple(range(devices)))


def exchange(slots, devices):
    return lax.all_to_all(
        slots,
        "dp",
        split_axis=0,
        concat_axis=0,
        tiled=True,
        axis_index_groups=[list(exchange_order(devices))],
    )


def dot_t(a, b):
    return lax.dot_general(a, b, (((1,), (1,)), ((), ())), preferred_element_type=jnp.float32)


def dot(a, b):
    return jnp.dot(a, b, preferred_element_type=jnp.float32)


def three_terms(value, lane, step):
    first = value.astype(jnp.bfloat16).astype(jnp.float32)
    rest = value - first
    second = rest.astype(jnp.bfloat16).astype(jnp.float32)
    third = jnp.where(lane < 3 * step, rest - second, 0.0)
    terms = jnp.where(lane < step, first, jnp.where(lane < 2 * step, second, third))
    return terms.astype(jnp.bfloat16)


def pack_queries(image_owner, step_queries, devices, capacity):
    rows = step_queries.shape[0]
    images = image_owner.shape[0] // devices
    slots = devices * capacity
    table = (rows // LANES + 1) * LANES

    def kernel(
        owner_hbm, query_hbm, packed, slot_out, owner, queries, row_of_slot, slot_of_row, in_sems, sems
    ):
        read_owner = pltpu.make_async_copy(owner_hbm, owner, in_sems.at[0])
        read_queries = pltpu.make_async_copy(query_hbm, queries, in_sems.at[1])
        read_owner.start()
        read_queries.start()
        base = lax.axis_index("dp") * rows
        for r in range(rows):
            slot_of_row[r] = -1
        for slot in range(slots):
            row_of_slot[slot] = 0
        read_owner.wait()
        copies = []
        for place, s in enumerate(exchange_order(devices)):
            rank = jnp.int32(0)
            for i in range(images):
                row = owner[s * images + i] - base
                local = jnp.logical_and(row >= 0, row < rows)
                slot = place * capacity + rank
                row_of_slot[jnp.where(local, slot, slots)] = row
                slot_of_row[jnp.where(local, row, rows)] = slot
                rank = rank + local.astype(jnp.int32)
            if place == 0:
                read_queries.wait()
            for k in range(capacity):
                slot = place * capacity + k
                copy = pltpu.make_async_copy(
                    queries.at[row_of_slot[slot]], packed.at[slot], sems.at[slot]
                )
                copy.start()
                copies.append(copy)
        write_slots = pltpu.make_async_copy(slot_of_row, slot_out, in_sems.at[2])
        write_slots.start()
        for copy in copies:
            copy.wait()
        write_slots.wait()

    return pl.pallas_call(
        kernel,
        in_specs=[pl.BlockSpec(memory_space=pl.ANY), pl.BlockSpec(memory_space=pl.ANY)],
        out_specs=[pl.BlockSpec(memory_space=pl.ANY), pl.BlockSpec(memory_space=pl.ANY)],
        out_shape=[
            jax.ShapeDtypeStruct((slots,) + step_queries.shape[1:], step_queries.dtype),
            jax.ShapeDtypeStruct((table,), jnp.int32),
        ],
        scratch_shapes=[
            pltpu.SMEM(image_owner.shape, jnp.int32),
            pltpu.VMEM(step_queries.shape, step_queries.dtype),
            pltpu.SMEM((slots + 1,), jnp.int32),
            pltpu.SMEM((table,), jnp.int32),
            pltpu.SemaphoreType.DMA((3,)),
            pltpu.SemaphoreType.DMA((slots,)),
        ],
        name="pack_queries",
    )(image_owner, step_queries)


def project(tokens, weight):
    count, depth = tokens.shape
    width = weight.shape[2] // 2
    columns = 2 * width + LANES
    sizes = [512, 512] + [1024] * ((depth - 1024) // 1024)
    starts = [sum(sizes[:c]) for c in range(len(sizes))]
    chunks = len(sizes)
    ahead = 3

    def kernel(
        token_hbm, weight_hbm, theirs_ref, ours_hbm, total_s, ours_s, token_s, weight_s, sems, out_sem
    ):
        mine = lax.axis_index("tensor")

        def lanes(half):
            return pl.ds(pl.multiple_of(half * width, width), width)

        def product(x, w):
            w = jnp.swapaxes(w, 0, 1)
            return dot(x, jnp.concatenate([w[0], w[1]], axis=1))

        loads = []
        for c in range(chunks):
            span = pl.ds(starts[c], sizes[c])
            loads.append(
                [
                    pltpu.make_async_copy(
                        token_hbm.at[:, span], token_s.at[:, span], sems.at[0, c]
                    ),
                    pltpu.make_async_copy(
                        weight_hbm.at[span, :, lanes(mine)], weight_s.at[0, span], sems.at[1, c]
                    ),
                ]
            )
        loads.append(
            [
                pltpu.make_async_copy(
                    weight_hbm.at[:, :, lanes(1 - mine)], weight_s.at[1], sems.at[2, 0]
                )
            ]
        )

        def start(c):
            if c < len(loads):
                for load in loads[c]:
                    load.start()

        for c in range(ahead):
            start(c)
        squares = jnp.zeros((count, LANES), jnp.float32)
        for c in range(chunks):
            for load in loads[c]:
                load.wait()
            start(c + ahead)
            span = slice(starts[c], starts[c] + sizes[c])
            x = token_s[:, span]
            part = product(x, weight_s[0, span])
            if c == 0:
                total_s[...] = part
            else:
                total_s[...] += part
            for lane in range(0, sizes[c], LANES):
                wide = x[:, lane : lane + LANES].astype(jnp.float32)
                squares += wide * wide
        squares = jnp.broadcast_to(jnp.sum(squares, axis=1, keepdims=True), (count, LANES))
        terms = three_terms(squares, lax.broadcasted_iota(jnp.int32, (count, LANES), 1), 1)
        ours_s[:, : 2 * width] = total_s[...].astype(jnp.bfloat16)
        ours_s[:, 2 * width :] = terms
        store = pltpu.make_async_copy(ours_s, ours_hbm.at[pl.ds(0, count)], out_sem)
        store.start()
        for load in loads[chunks]:
            load.wait()
        theirs_ref[:, : 2 * width] = product(token_s[...], weight_s[1]).astype(jnp.bfloat16)
        theirs_ref[:, 2 * width :] = terms
        store.wait()

    hbm = pl.BlockSpec(memory_space=pltpu.HBM)
    return pl.pallas_call(
        kernel,
        in_specs=[hbm, hbm],
        out_specs=[pl.BlockSpec(memory_space=pltpu.VMEM), pl.BlockSpec(memory_space=pl.ANY)],
        out_shape=[
            jax.ShapeDtypeStruct((count, columns), jnp.bfloat16),
            jax.ShapeDtypeStruct((FAR_BYTES // (2 * columns), columns), jnp.bfloat16),
        ],
        scratch_shapes=[
            pltpu.VMEM((count, 2 * width), jnp.float32),
            pltpu.VMEM((count, columns), jnp.bfloat16),
            pltpu.VMEM(tokens.shape, tokens.dtype),
            pltpu.VMEM((2, depth, 2, width), weight.dtype),
            pltpu.SemaphoreType.DMA((3, chunks)),
            pltpu.SemaphoreType.DMA,
        ],
        compiler_params=pltpu.CompilerParams(vmem_limit_bytes=60 << 20),
        cost_estimate=pl.CostEstimate(flops=1 << 20, bytes_accessed=1 << 16, transcendentals=0),
        name="project",
    )(tokens, weight)


def cached_attention(queries, cache_keys, cache_values, step_keys, step_values, lengths):
    rows, context, width = cache_keys.shape
    kv_local = width // HD
    heads = queries.shape[2] // HD
    group = heads // kv_local
    stacked = group * STEPS
    block = 8 if rows % 8 == 0 else 2
    scale = HD**-0.5

    def kernel(length_ref, q_ref, k_ref, v_ref, sk_ref, sv_ref, out_ref, q_s, sk_s, sv_s):
        first = pl.program_id(0) * block
        for r in range(block):
            for g in range(kv_local):
                sk_s[g, r * STEPS : (r + 1) * STEPS, :] = sk_ref[
                    r, :, g * HD : (g + 1) * HD
                ].astype(jnp.float32)
                sv_s[g, r * STEPS : (r + 1) * STEPS, :] = sv_ref[
                    r, :, g * HD : (g + 1) * HD
                ].astype(jnp.float32)
                for j in range(group):
                    h = g * group + j
                    at = r * stacked + j * STEPS
                    q_s[g, at : at + STEPS, :] = q_ref[r, :, h * HD : (h + 1) * HD].astype(
                        jnp.float32
                    )
        lane = lax.broadcasted_iota(jnp.int32, (STEPS, LANES), 1)
        logs = [jnp.zeros((STEPS, LANES), jnp.float32) for _ in range(block)]
        for g in range(kv_local):
            q = q_s[g].astype(jnp.bfloat16)
            steps = dot_t(q, sk_s[g].astype(jnp.bfloat16)) * scale
            at_row = lax.broadcasted_iota(jnp.int32, steps.shape, 0)
            at_key = lax.broadcasted_iota(jnp.int32, steps.shape, 1)
            own = (at_row // stacked == at_key // STEPS) & (at_key % STEPS <= at_row % STEPS)
            steps = jnp.where(own, steps, FLOOR)
            step_peak = jnp.max(steps, axis=1, keepdims=True)
            scores = []
            position = lax.broadcasted_iota(jnp.int32, (stacked, context), 1)
            for r in range(block):
                part = dot_t(q[r * stacked : (r + 1) * stacked], k_ref[r, :, g * HD : (g + 1) * HD])
                scores.append(jnp.where(position < length_ref[first + r], part * scale, FLOOR))
            cached = jnp.concatenate(scores, axis=0)
            peak = jnp.maximum(jnp.max(cached, axis=1, keepdims=True), step_peak)
            cached = jnp.exp(cached - peak)
            steps = jnp.where(own, jnp.exp(steps - peak), 0.0)
            total = jnp.sum(cached, axis=1, keepdims=True) + jnp.sum(steps, axis=1, keepdims=True)
            cached = cached.astype(jnp.bfloat16)
            mixed = dot(steps.astype(jnp.bfloat16), sv_s[g].astype(jnp.bfloat16))
            inverse = 1.0 / total
            log = jnp.broadcast_to(peak + jnp.log(total), (block * stacked, LANES))
            for r in range(block):
                span = slice(r * stacked, (r + 1) * stacked)
                part = dot(cached[span], v_ref[r, :, g * HD : (g + 1) * HD])
                part = (part + mixed[span]) * inverse[span]
                for j in range(group):
                    h = g * group + j
                    head = slice(j * STEPS, (j + 1) * STEPS)
                    out_ref[r * STEPS : (r + 1) * STEPS, h * HD : (h + 1) * HD] = part[head]
                    at = r * stacked + j * STEPS
                    logs[r] = jnp.where(lane == h, log[at : at + STEPS], logs[r])
        for r in range(block):
            out_ref[r * STEPS : (r + 1) * STEPS, heads * HD :] = logs[r]

    def spec(array):
        return pl.BlockSpec((block,) + array.shape[1:], lambda i, length_ref: (i, 0, 0))

    return pl.pallas_call(
        kernel,
        grid_spec=pltpu.PrefetchScalarGridSpec(
            num_scalar_prefetch=1,
            grid=(rows // block,),
            in_specs=[
                spec(queries),
                spec(cache_keys),
                spec(cache_values),
                spec(step_keys),
                spec(step_values),
            ],
            out_specs=pl.BlockSpec(
                (block * STEPS, heads * HD + LANES), lambda i, length_ref: (i, 0)
            ),
            scratch_shapes=[
                pltpu.VMEM((kv_local, block * stacked, HD), jnp.float32),
                pltpu.VMEM((kv_local, block * STEPS, HD), jnp.float32),
                pltpu.VMEM((kv_local, block * STEPS, HD), jnp.float32),
            ],
        ),
        out_shape=jax.ShapeDtypeStruct(
            (FAR_BYTES // (4 * (heads * HD + LANES)), heads * HD + LANES), jnp.float32
        ),
        compiler_params=pltpu.CompilerParams(vmem_limit_bytes=60 << 20),
        cost_estimate=pl.CostEstimate(flops=1 << 20, bytes_accessed=1 << 16, transcendentals=0),
        name="cached_attention",
    )(lengths, queries, cache_keys, cache_values, step_keys, step_values)


def visual_attention(places, queries, ours, received):
    images = places.shape[0] // 4
    slots, _, full = queries.shape
    heads = full // HD
    columns = ours.shape[1]
    split = columns - LANES
    kv_local = split // (2 * HD)
    count = received.shape[0]
    run = count // RUNS
    group = heads // kv_local
    stacked = group * STEPS
    window = VMAX + 16
    scale = HD**-0.5

    def kernel(
        place_hbm,
        q_ref,
        received_ref,
        ours_hbm,
        out_hbm,
        place_ref,
        ours_s,
        pair_ref,
        q_s,
        score_s,
        weight_s,
        out_ref,
        place_sem,
        load_sems,
        sems,
    ):
        read_places = pltpu.make_async_copy(place_hbm, place_ref, place_sem)
        read_places.start()
        loads = []
        for k in range(RUNS):
            rows = pl.ds(k * run, run)
            load = pltpu.make_async_copy(ours_hbm.at[rows], ours_s.at[rows], load_sems.at[k])
            load.start()
            loads.append(load)
        stores = []
        read_places.wait()
        for i in range(images):
            slot = place_ref[0 * images + i]
            for h in range(heads):
                q_s[i, h * STEPS : (h + 1) * STEPS, :] = q_ref[
                    slot, :, h * HD : (h + 1) * HD
                ].astype(jnp.float32)
        for k in range(RUNS):
            loads[k].wait()
            rows = slice(k * run, (k + 1) * run)
            squares = ours_s[rows, split:].astype(jnp.float32) + received_ref[
                rows, split:
            ].astype(jnp.float32)
            factor = lax.rsqrt(jnp.sum(squares, axis=1, keepdims=True) / D + EPSILON)
            for at in range(0, split, LANES):
                lanes = slice(at, at + LANES)
                total = ours_s[rows, lanes].astype(jnp.float32) + received_ref[rows, lanes].astype(
                    jnp.float32
                )
                pair_ref[rows, lanes] = (total * factor).astype(pair_ref.dtype)
        for i in range(images):
            rows = pl.ds(pl.multiple_of(place_ref[1 * images + i], 16), window)
            q = q_s[i].astype(jnp.bfloat16)
            for g in range(kv_local):
                score_s[i, g * stacked : (g + 1) * stacked, :] = dot_t(
                    q[g * stacked : (g + 1) * stacked], pair_ref[rows, g * HD : (g + 1) * HD]
                )
        column = lax.broadcasted_iota(jnp.int32, (heads * STEPS, window), 1)
        inverses = []
        logs = []
        for i in range(images):
            start = place_ref[2 * images + i]
            live = (column >= start) & (column < start + place_ref[3 * images + i])
            scores = jnp.where(live, score_s[i] * scale, FLOOR)
            peak = jnp.max(scores, axis=1, keepdims=True)
            weights = jnp.exp(scores - peak)
            total = jnp.sum(weights, axis=1, keepdims=True)
            weight_s[i] = weights.astype(jnp.bfloat16)
            inverses.append(1.0 / total)
            logs.append(jnp.broadcast_to(peak + jnp.log(total), (heads * STEPS, LANES)))
        lane = lax.broadcasted_iota(jnp.int32, (STEPS, LANES), 1)
        for i in range(images):
            rows = pl.ds(pl.multiple_of(place_ref[1 * images + i], 16), window)
            for g in range(kv_local):
                at = (kv_local + g) * HD
                part = dot(
                    weight_s[i, g * stacked : (g + 1) * stacked, :], pair_ref[rows, at : at + HD]
                )
                part = part * inverses[i][g * stacked : (g + 1) * stacked]
                for j in range(group):
                    h = g * group + j
                    out_ref[i, :, h * HD : (h + 1) * HD] = part[
                        j * STEPS : (j + 1) * STEPS
                    ].astype(out_ref.dtype)
            packed = jnp.zeros((STEPS, LANES), jnp.float32)
            for h in range(heads):
                log = logs[i][h * STEPS : (h + 1) * STEPS]
                packed = jnp.where(lane % heads == h, log, packed)
            out_ref[i, :, full:] = three_terms(packed, lane, heads)
            store = pltpu.make_async_copy(out_ref.at[i], out_hbm.at[place_ref[0 * images + i]], sems.at[i])
            store.start()
            stores.append(store)
        for store in stores:
            store.wait()

    anywhere = pl.BlockSpec(memory_space=pl.ANY)
    vmem = pl.BlockSpec(memory_space=pltpu.VMEM)
    return pl.pallas_call(
        kernel,
        in_specs=[
            anywhere,
            vmem,
            vmem,
            anywhere,
        ],
        out_specs=anywhere,
        out_shape=jax.ShapeDtypeStruct((slots, STEPS, full + LANES), queries.dtype),
        scratch_shapes=[
            pltpu.SMEM(places.shape, jnp.int32),
            pltpu.VMEM((count, columns), jnp.bfloat16),
            pltpu.VMEM((count, split), jnp.bfloat16),
            pltpu.VMEM((images, heads * STEPS, HD), jnp.float32),
            pltpu.VMEM((images, heads * STEPS, window), jnp.float32),
            pltpu.VMEM((images, heads * STEPS, window), jnp.bfloat16),
            pltpu.VMEM((images, STEPS, full + LANES), queries.dtype),
            pltpu.SemaphoreType.DMA,
            pltpu.SemaphoreType.DMA((RUNS,)),
            pltpu.SemaphoreType.DMA((images,)),
        ],
        compiler_params=pltpu.CompilerParams(vmem_limit_bytes=32 << 20),
        name="visual_attention",
    )(places, queries, received, ours)


def merge(slot_of_row, returned, cached, rows):
    full = cached.shape[1] - LANES
    heads = full // HD
    count = rows * STEPS
    block = 2 * STEPS
    runs = 3 if rows % 6 == 0 else 1
    run = count // runs

    def kernel(
        slot_hbm, returned_ref, cached_hbm, out_hbm, slot_ref, cached_s, other_s, out_s, slot_sem, sems
    ):
        read_slots = pltpu.make_async_copy(slot_hbm, slot_ref, slot_sem)
        read_slots.start()
        loads = []
        for k in range(runs):
            span = pl.ds(k * run, run)
            load = pltpu.make_async_copy(cached_hbm.at[span], cached_s.at[span], sems.at[0, k])
            load.start()
            loads.append(load)
        read_slots.wait()
        for r in range(rows):
            present = slot_ref[r] >= 0
            other = returned_ref[jnp.maximum(slot_ref[r], 0)].astype(jnp.float32)
            span = slice(r * STEPS, (r + 1) * STEPS)
            other_s[span, :full] = jnp.where(present, other[:, :full], 0.0)
            other_s[span, full:] = jnp.where(present, other[:, full:], FLOOR)
        stores = []
        for k in range(runs):
            loads[k].wait()
            for at in range(k * run, (k + 1) * run, block):
                span = slice(at, at + block)
                terms = other_s[span, full:]
                log = (
                    terms[:, :heads] + terms[:, heads : 2 * heads] + terms[:, 2 * heads : 3 * heads]
                )
                share = 1.0 / (1.0 + jnp.exp(cached_s[span, full : full + heads] - log))
                for h in range(heads):
                    lanes = slice(h * HD, (h + 1) * HD)
                    own = cached_s[span, lanes]
                    mixed = own + share[:, h : h + 1] * (other_s[span, lanes] - own)
                    mixed = mixed.astype(out_s.dtype).reshape(block // STEPS, STEPS, HD)
                    out_s[at // STEPS : (at + block) // STEPS, :, lanes] = mixed
            span = pl.ds(k * run // STEPS, run // STEPS)
            store = pltpu.make_async_copy(out_s.at[span], out_hbm.at[span], sems.at[1, k])
            store.start()
            stores.append(store)
        for store in stores:
            store.wait()

    anywhere = pl.BlockSpec(memory_space=pl.ANY)
    return pl.pallas_call(
        kernel,
        in_specs=[anywhere, pl.BlockSpec(memory_space=pltpu.VMEM), anywhere],
        out_specs=anywhere,
        out_shape=jax.ShapeDtypeStruct((rows, STEPS, full), jnp.bfloat16),
        scratch_shapes=[
            pltpu.SMEM(slot_of_row.shape, jnp.int32),
            pltpu.VMEM((count, full + LANES), jnp.float32),
            pltpu.VMEM((count, full + LANES), jnp.float32),
            pltpu.VMEM((rows, STEPS, full), jnp.bfloat16),
            pltpu.SemaphoreType.DMA,
            pltpu.SemaphoreType.DMA((2, runs)),
        ],
        compiler_params=pltpu.CompilerParams(vmem_limit_bytes=32 << 20),
        name="merge",
    )(slot_of_row, returned, cached)


def shards(
    visual_tokens,
    kv_weight,
    image_lengths,
    image_owner,
    cache_lengths,
    cache_keys,
    cache_values,
    step_queries,
    step_keys,
    step_values,
):
    devices = lax.axis_size("dp")
    rows_local = cache_lengths.shape[0]
    images_local = image_lengths.shape[1]
    capacity = -(-rows_local // devices)
    weight_half = kv_weight[0]
    packed, slot_of_row = pack_queries(image_owner, step_queries, devices, capacity)
    tokens, packed = lax.optimization_barrier((visual_tokens, packed))
    asked = exchange(packed, devices)
    for_partner, ours = project(tokens, weight_half)
    from_partner = lax.ppermute(for_partner, "tensor", [(0, 1), (1, 0)])

    cached = cached_attention(
        step_queries, cache_keys, cache_values, step_keys, step_values, cache_lengths
    )

    device = lax.axis_index("dp")
    own_lengths = lax.dynamic_index_in_dim(image_lengths, device, 0, keepdims=False)
    own_device = (
        lax.dynamic_slice_in_dim(image_owner, device * images_local, images_local) // rows_local
    )
    order = jnp.arange(images_local)
    earlier = order[None, :] < order[:, None]
    own_rank = jnp.sum(
        ((own_device[:, None] == own_device[None, :]) & earlier).astype(jnp.int32), axis=1
    )
    starts = jnp.sum(jnp.where(earlier, own_lengths[None, :], 0), axis=1)
    window_at = jnp.minimum(starts // 16 * 16, visual_tokens.shape[0] - VMAX - 16)
    order_of_place = jnp.array(exchange_order(devices), jnp.int32)
    own_place = jnp.sum(
        jnp.where(own_device[:, None] == order_of_place[None, :], jnp.arange(devices)[None, :], 0),
        axis=1,
    )
    places = jnp.concatenate(
        [own_place * capacity + own_rank, window_at, starts - window_at, own_lengths]
    )

    answers = visual_attention(places, asked, ours, from_partner)
    returned = exchange(answers, devices)
    return merge(slot_of_row, returned, cached, rows_local)


def solution(mesh):
    return jax.shard_map(
        shards,
        mesh=mesh,
        in_specs=(
            P(("groups", "dp"), "tensor"),
            P("tensor", None, None, None),
            P("groups", None),
            P("groups"),
            P(("groups", "dp")),
            P(("groups", "dp"), None, "tensor"),
            P(("groups", "dp"), None, "tensor"),
            P(("groups", "dp"), None, "tensor"),
            P(("groups", "dp"), None, "tensor"),
            P(("groups", "dp"), None, "tensor"),
        ),
        out_specs=P(("groups", "dp"), None, "tensor"),
        check_vma=False,
    )
```
